32 devices in a mesh: seq: 16 (over z, y, x), head: 2 (over core).
Axes of the slice: x: 2, y: 2, z: 4, core: 2. Of those that a mesh axis runs over, the one named last changes fastest.
Arguments:
- hidden_in: bfloat16 [2048, 2048], P(('seq', 'head')), may hold values from -6 to 6
- w_inner: bfloat16 [2048, 4096], P(None, 'head'), may hold values from -0.125 to 0.125
- w_inout: bfloat16 [2048, 512], replicated, may hold values from -0.0078125 to 0.0078125
- w_step: bfloat16 [2, 2048, 64], P(None, None, 'head'), may hold values from -0.125 to 0.125
- step_bias: float32 [2, 64], P(None, 'head'), may hold values from -1 to 1
- decay_rate: float32 [64], P('head'), may hold values from 2e-05 to 0.05
- skip_gain: float32 [64], P('head'), may hold values from 0.5 to 1.5
Outputs:
- mixed: bfloat16 [2048, 4096], P('seq', 'head')
The draws below stay inside these ranges and needn't reach their ends.
All inputs are finite; a program needn't handle non-finite values.
Results may differ from the reference program's by a relative error of at most 0.0052.
Values may be sent and summed in bfloat16 or wider, within the bound.
A program may use at most 128 MiB of HBM per device.

```python
import math
import jax
import jax.numpy as jnp
from jax import lax

DMODEL = 2048
HEADS = 64
HEADDIM = 64
STATE = 128
SPAN = 128
DINNER = 4096
TOKENS = 2048


def steps_of(stream_key, shape, split, smallest, largest):
    loudness, own = 1.0, jax.random.fold_in(stream_key, 6)
    for dim, shards_of in split:
        steps = jnp.exp(jax.random.uniform(jax.random.fold_in(own, dim), (shards_of,), jnp.float32, smallest / len(split), largest / len(split)))
        loudness = loudness * jnp.repeat(steps, shape[dim] // shards_of).reshape([-1 if axis == dim else 1 for axis in range(len(shape))])
    return loudness


def normal_values(own_key, shape, scale, limit, cuts=(), dtype=jnp.bfloat16):
    result = jax.random.normal(own_key, shape, jnp.float32) * scale
    if len(cuts) > 0:
        result = steps_of(own_key, shape, cuts, -0.22, 0.18) * result
    return jnp.clip(result, min=-limit, max=limit).astype(dtype)


def setup_inputs(seed: int = 0) -> dict:
    key_of = jax.random.split(jax.random.key(seed), 8)
    return {
        "hidden_in": normal_values(key_of[0], (TOKENS, DMODEL), 1.0, 6.0, ((0, 32),)),
        "w_inner": normal_values(key_of[1], (DMODEL, DINNER), DMODEL ** -0.5, 0.125, ((1, 2),)),
        "w_inout": normal_values(key_of[2], (DMODEL, 4 * STATE), (DMODEL * TOKENS // 8) ** -0.5, 0.0078125),
        "w_step": normal_values(key_of[3], (2, DMODEL, HEADS), DMODEL ** -0.5, 0.125, ((2, 2),)),
        "step_bias": jnp.clip(jax.random.uniform(key_of[4], (2, HEADS), jnp.float32, -1.0, 1.0) * steps_of(key_of[4], (2, HEADS), ((1, 2),), -0.4, 0.0), -1.0, 1.0),
        "decay_rate": jnp.clip(jnp.exp(math.log(0.05) - 7.824046 * jax.random.uniform(key_of[5], (HEADS,), jnp.float32) ** steps_of(key_of[5], (HEADS,), ((0, 2),), -0.2, 0.2)), 1.9999999494757503e-05, 0.05),
        "skip_gain": jnp.clip(0.5 + 1.0 * jax.random.uniform(key_of[6], (HEADS,), jnp.float32) ** steps_of(key_of[6], (HEADS,), ((0, 2),), -0.2, 0.2), 0.5, 1.5),
    }


def span_pass(inner, in_map, out_map, steps, rate):
    rows, heads_here, width = inner.shape
    count = rows // SPAN
    states = in_map.shape[1]
    exact = lax.Precision.HIGHEST
    values = inner.astype(jnp.float32).reshape(count, SPAN, heads_here, width)
    in_blocks = in_map.astype(jnp.float32).reshape(count, SPAN, states)
    out_blocks = out_map.astype(jnp.float32).reshape(count, SPAN, states)
    logs = (-steps * rate[None, :]).reshape(count, SPAN, heads_here).transpose(0, 2, 1)
    step_blocks = steps.reshape(count, SPAN, heads_here).transpose(0, 2, 1)
    cums = jnp.cumsum(logs, axis=2)
    scores = jnp.einsum('kin,kjn->kij', out_blocks, in_blocks, precision=exact)
    spread = cums[:, :, :, None] - cums[:, :, None, :]
    lower = jnp.arange(SPAN)[:, None] > jnp.arange(SPAN)[None, :]
    decay = jnp.where(lower, jnp.exp(jnp.where(lower, spread, 0.0)), 0.0)
    weights = decay * scores[:, None, :, :] * step_blocks[:, :, None, :]
    intra = jnp.einsum('khij,kjhp->kihp', weights, values, precision=exact)
    tail = jnp.exp(cums[:, :, -1:] - cums) * step_blocks
    pieces = jnp.einsum('khj,kjn,kjhp->khnp', tail, in_blocks, values, precision=exact)
    totals = cums[:, :, -1]

    def advance(carry, item):
        total, piece = item
        return jnp.exp(total)[:, None, None] * carry + piece, carry

    last, starts = lax.scan(advance, jnp.zeros((heads_here, states, width), jnp.float32), (totals, pieces))
    inter = jnp.einsum('khi,kin,khnp->kihp', jnp.exp(cums), out_blocks, starts, precision=exact)
    return (intra + inter).reshape(rows, heads_here, width), last


def reference(hidden_in, w_inner, w_inout, w_step, step_bias, decay_rate, skip_gain):
    inner = jnp.dot(hidden_in, w_inner, preferred_element_type=jnp.float32).astype(jnp.bfloat16)
    inner = inner.reshape(TOKENS, HEADS, HEADDIM)
    maps = jnp.dot(hidden_in, w_inout, preferred_element_type=jnp.float32).astype(jnp.bfloat16)
    in_fwd = maps[:, :STATE]
    out_fwd = maps[:, STATE:2 * STATE]
    in_bwd = maps[:, 2 * STATE:3 * STATE]
    out_bwd = maps[:, 3 * STATE:]
    step_fwd = jax.nn.softplus(jnp.dot(hidden_in, w_step[0], preferred_element_type=jnp.float32) + step_bias[0][None, :])
    step_bwd = jax.nn.softplus(jnp.dot(hidden_in, w_step[1], preferred_element_type=jnp.float32) + step_bias[1][None, :])

    def per_head(item):
        values, forward_steps, backward_steps, rate = item
        ahead = span_pass(values, in_fwd, out_fwd, forward_steps, rate)[0]
        behind = span_pass(jnp.flip(values, 0), jnp.flip(in_bwd, 0), jnp.flip(out_bwd, 0), jnp.flip(backward_steps, 0), rate)[0]
        return ahead + jnp.flip(behind, 0)

    mixed = lax.map(per_head, (inner.transpose(1, 0, 2)[:, :, None, :], step_fwd.T[:, :, None], step_bwd.T[:, :, None], decay_rate[:, None]))
    mixed = mixed[:, :, 0, :].transpose(1, 0, 2)
    mixed = mixed + skip_gain[None, :, None] * inner.astype(jnp.float32)
    return mixed.reshape(TOKENS, DINNER).astype(jnp.bfloat16)
```

```python
import functools

import jax
import jax.numpy as jnp
from jax import lax
from jax.experimental import pallas as pl
from jax.experimental.pallas import tpu as pltpu
from jax.sharding import PartitionSpec as P

HEADDIM = 64
GROUP = 4
MESH = pl.DeviceIdType.MESH
F32 = jnp.float32
BF16 = jnp.bfloat16
EXACT = lax.Precision.HIGHEST


def bdot(a, b):
    return jnp.dot(a, b, preferred_element_type=F32)


def turned(a, b):
    return lax.dot_general(
        a, b, (((0,), (0,)), ((), ())), precision=EXACT, preferred_element_type=F32
    )


def softplus(x):
    return jnp.maximum(x, 0.0) + jnp.log1p(jnp.exp(-jnp.abs(x)))


def kernel(
    ns, nh, rows, dim, width, heads, states, tile, chunk,
    x_ref, w_hbm, wio_hbm, ws_ref, bias_ref, rate_ref, skip_ref, out_ref,
    hid, w_ref, wio_ref, inn, st_f, st_b, tot_f, tot_b, own_out, own_scale, acc,
    snd_f, snd_b, rcv_f, rcv_b,
    w_sem, wio_sem, x_sem, peer_send, peer_recv, sib_send, sib_recv,
    fs_sem, fr_sem, bs_sem, br_sem,
):
    s = lax.axis_index("seq")
    h = lax.axis_index("head")
    span = rows * nh
    place = lax.rem(s, GROUP)
    lap = lax.div(s, GROUP)
    laps = ns // GROUP
    first_seq = s - place
    tiles = width // tile
    chunks = width // chunk

    def partner(d):
        px = lax.rem(lax.rem(place, 2) + d % 2, 2)
        py = lax.rem(lax.div(place, 2) + d // 2, 2)
        return py * 2 + px

    def sibling(e):
        return lax.rem(h + e, nh)

    def piece(g, hh):
        return pl.ds(pl.multiple_of((g * nh + hh) * rows, rows), rows)

    w_copies = [
        pltpu.make_async_copy(
            w_hbm.at[:, pl.ds(t * tile, tile)], w_ref.at[:, pl.ds(t * tile, tile)], w_sem.at[t]
        )
        for t in range(tiles)
    ]
    own_copy = pltpu.make_async_copy(x_ref, hid.at[piece(place, h)], x_sem)
    own_copy.start()
    wio_copy = pltpu.make_async_copy(wio_hbm, wio_ref, wio_sem)
    wio_copy.start()
    for c in w_copies:
        c.start()

    barrier = pltpu.get_barrier_semaphore()
    for d in range(1, GROUP):
        pl.semaphore_signal(barrier, 1, device_id=(first_seq + partner(d), h), device_id_type=MESH)
    for e in range(1, nh):
        pl.semaphore_signal(barrier, 1, device_id=(s, sibling(e)), device_id_type=MESH)

    @pl.when(lap > 0)
    def _():
        pl.semaphore_signal(barrier, 1, device_id=(s - GROUP, h), device_id_type=MESH)

    @pl.when(lap < laps - 1)
    def _():
        pl.semaphore_signal(barrier, 1, device_id=(s + GROUP, h), device_id_type=MESH)

    near = jnp.where(lap > 0, 1, 0) + jnp.where(lap < laps - 1, 1, 0)
    pl.semaphore_wait(barrier, GROUP - 1 + nh - 1 + near)

    peers = [
        pltpu.make_async_remote_copy(
            src_ref=x_ref,
            dst_ref=hid.at[piece(place, h)],
            send_sem=peer_send.at[d - 1],
            recv_sem=peer_recv.at[d - 1],
            device_id=(first_seq + partner(d), h),
            device_id_type=MESH,
        )
        for d in range(1, GROUP)
    ]

    def sib_copies(d):
        src = x_ref if d == 0 else hid.at[piece(partner(d), h)]
        return [
            pltpu.make_async_remote_copy(
                src_ref=src,
                dst_ref=hid.at[piece(partner(d), h)],
                send_sem=sib_send.at[d * (nh - 1) + e - 1],
                recv_sem=sib_recv.at[d * (nh - 1) + e - 1],
                device_id=(s, sibling(e)),
                device_id_type=MESH,
            )
            for e in range(1, nh)
        ]

    sibs = [sib_copies(d) for d in range(GROUP)]
    for c in sibs[0]:
        c.start()
    for c in peers:
        c.start()

    @pl.when(lap == 0)
    def _():
        rcv_f[...] = jnp.zeros_like(rcv_f)

    @pl.when(lap == laps - 1)
    def _():
        rcv_b[...] = jnp.zeros_like(rcv_b)

    below = lax.broadcasted_iota(jnp.int32, (span, span), 0)
    right = lax.broadcasted_iota(jnp.int32, (span, span), 1)
    left_half = lax.broadcasted_iota(jnp.int32, (1, 128), 1) < HEADDIM
    tri = jnp.where(below >= right, 1.0, 0.0).astype(F32)
    rate = rate_ref[...]

    def pair(v, i):
        return jnp.where(left_half, v[:, 2 * i : 2 * i + 1], v[:, 2 * i + 1 : 2 * i + 2])

    def spread_row(v, k):
        n = chunk // 128
        return jnp.concatenate([pair(v, k * n + i) for i in range(n)], axis=1)

    def block(g, waits):
        xb = hid[pl.ds(pl.multiple_of(g * span, span), span), :]
        if waits:
            wio_copy.wait()
        maps = bdot(xb, wio_ref[...]).astype(BF16)
        step_f = softplus(bdot(xb, ws_ref[0]) + bias_ref[0:1, :])
        step_b = softplus(bdot(xb, ws_ref[1]) + bias_ref[1:2, :])
        log_f = -rate * step_f
        log_b = -rate * step_b
        cum_f = jnp.dot(tri, log_f, precision=EXACT, preferred_element_type=F32)
        cum_b = jnp.dot(tri, log_b, precision=EXACT, preferred_element_type=F32)
        exc_b = cum_b - log_b
        last_f = cum_f[span - 1 : span, :]
        last_b = cum_b[span - 1 : span, :]
        tot_f[g] = jnp.broadcast_to(last_f, (8, heads))
        tot_b[g] = jnp.broadcast_to(last_b, (8, heads))
        tail_f = jnp.exp(last_f - cum_f) * step_f
        tail_b = jnp.exp(exc_b) * step_b
        in_f = maps[:, :states].astype(F32).T.astype(BF16)
        in_b = maps[:, 2 * states : 3 * states].astype(F32).T.astype(BF16)
        per = tile // 128
        for t in range(tiles):
            if waits:
                w_copies[t].wait()
            values = bdot(xb, w_ref[:, t * tile : (t + 1) * tile]).astype(BF16)
            inn[:, t * tile : (t + 1) * tile] = values
            wide = values.astype(F32)
            ahead = jnp.concatenate([pair(tail_f, t * per + i) for i in range(per)], axis=1)
            behind = jnp.concatenate([pair(tail_b, t * per + i) for i in range(per)], axis=1)
            st_f[g, :, t * tile : (t + 1) * tile] = bdot(in_f, (ahead * wide).astype(BF16))
            st_b[g, :, t * tile : (t + 1) * tile] = bdot(in_b, (behind * wide).astype(BF16))
        return maps, step_f, step_b, cum_f, exc_b, last_b

    def forward(d):
        peers[d - 1].wait_recv()
        for c in sibs[d]:
            c.start()

    own_copy.wait()
    for c in sibs[0]:
        c.wait_recv()
    maps, step_f, step_b, cum_f, exc_b, last_b = block(place, True)
    forward(1)

    out_f = maps[:, states : 2 * states]
    out_b = maps[:, 3 * states :]
    own_out[0] = out_f
    own_out[1] = out_b
    own_scale[0] = jnp.exp(cum_f)
    own_scale[1] = jnp.exp(last_b - exc_b)
    lower = below > right
    contract = (((1,), (1,)), ((), ()))
    score = jnp.where(
        lower,
        lax.dot_general(out_f, maps[:, :states], contract, preferred_element_type=F32),
        lax.dot_general(
            out_b, maps[:, 2 * states : 3 * states], contract, preferred_element_type=F32
        ),
    )
    score = jnp.where(below == right, 0.0, score)
    unit = jnp.where(below == right, 1.0, 0.0).astype(F32)
    cum_row = turned(cum_f, unit)
    exc_row = turned(exc_b, unit)
    step_row_f = turned(step_f, unit)
    step_row_b = turned(step_b, unit)
    skip = skip_ref[...]
    for i in range(heads // 2):
        both = inn[:, i * 128 : (i + 1) * 128]
        parts = []
        for k in (2 * i, 2 * i + 1):
            gap = jnp.where(
                lower,
                cum_f[:, k : k + 1] - cum_row[k : k + 1, :],
                exc_row[k : k + 1, :] - exc_b[:, k : k + 1],
            )
            scale = jnp.where(lower, step_row_f[k : k + 1, :], step_row_b[k : k + 1, :])
            parts.append(bdot((jnp.exp(gap) * (score * scale)).astype(BF16), both))
        acc[:, i * 128 : (i + 1) * 128] = (
            jnp.where(left_half, parts[0], parts[1]) + pair(skip, i) * both.astype(F32)
        )

    for d in range(1, GROUP):
        for c in sibs[d]:
            c.wait_recv()
        if d < GROUP - 1:
            forward(d + 1)
        block(partner(d), False)

    tf = [tot_f[b][0:1, :] for b in range(GROUP)]
    tb = [tot_b[b][0:1, :] for b in range(GROUP)]
    none = jnp.zeros_like(tf[0])

    def between(logs, keep):
        return jnp.exp(sum([jnp.where(keep(b), logs[b], none) for b in range(GROUP)], none))

    all_f = [between(tf, lambda c, b=b: jnp.asarray(c > b)) for b in range(GROUP)]
    all_b = [between(tb, lambda c, b=b: jnp.asarray(c < b)) for b in range(GROUP)]
    whole_f = between(tf, lambda c: jnp.asarray(True))
    whole_b = between(tb, lambda c: jnp.asarray(True))
    mine_f = [
        jnp.where(b < place, between(tf, lambda c, b=b: (c > b) & (c < place)), none)
        for b in range(GROUP)
    ]
    mine_b = [
        jnp.where(b > place, between(tb, lambda c, b=b: (c < b) & (c > place)), none)
        for b in range(GROUP)
    ]
    reach_f = between(tf, lambda c: c < place)
    reach_b = between(tb, lambda c: c > place)

    f_copies = [
        pltpu.make_async_remote_copy(
            src_ref=snd_f.at[k], dst_ref=rcv_f.at[k], send_sem=fs_sem.at[k], recv_sem=fr_sem.at[k],
            device_id=(s + GROUP, h), device_id_type=MESH,
        )
        for k in range(chunks)
    ]
    b_copies = [
        pltpu.make_async_remote_copy(
            src_ref=snd_b.at[k], dst_ref=rcv_b.at[k], send_sem=bs_sem.at[k], recv_sem=br_sem.at[k],
            device_id=(s - GROUP, h), device_id_type=MESH,
        )
        for k in range(chunks)
    ]

    def step(k, st, rcv, snd, copies, got, sent, totals, whole, mine, reach):
        cols = slice(k * chunk, (k + 1) * chunk)

        @pl.when(got)
        def _():
            copies[k].wait_recv()

        @pl.when(sent)
        def _():
            total = spread_row(whole, k) * rcv[k].astype(F32)
            for b in range(GROUP):
                total = total + spread_row(totals[b], k) * st[b, :, cols]
            snd[k] = total.astype(BF16)
            copies[k].start()

        carry = spread_row(reach, k) * rcv[k].astype(F32)
        for b in range(GROUP):
            carry = carry + spread_row(mine[b], k) * st[b, :, cols]
        return carry.astype(BF16)

    for k in range(chunks):
        cols = slice(k * chunk, (k + 1) * chunk)
        ahead = step(
            k, st_f, rcv_f, snd_f, f_copies, lap > 0, lap < laps - 1, all_f, whole_f, mine_f, reach_f
        )
        behind = step(
            k, st_b, rcv_b, snd_b, b_copies, lap < laps - 1, lap > 0, all_b, whole_b, mine_b, reach_b
        )
        result = acc[:, cols] + spread_row(own_scale[0], k) * bdot(own_out[0], ahead)
        result = result + spread_row(own_scale[1], k) * bdot(own_out[1], behind)
        out_ref[:, cols] = result.astype(out_ref.dtype)

    for c in peers:
        c.wait_send()
    for group in sibs:
        for c in group:
            c.wait_send()

    @pl.when(lap < laps - 1)
    def _():
        for c in f_copies:
            c.wait_send()

    @pl.when(lap > 0)
    def _():
        for c in b_copies:
            c.wait_send()


def shards(ns, nh, hidden_in, w_inner, w_inout, w_step, step_bias, decay_rate, skip_gain):
    rows, dim = hidden_in.shape
    width = w_inner.shape[1]
    heads = w_step.shape[2]
    states = w_inout.shape[1] // 4
    span = rows * nh
    tile = 256
    chunk = 256
    tiles, chunks = width // tile, width // chunk
    dma = pltpu.SemaphoreType.DMA
    vmem = pl.BlockSpec(memory_space=pltpu.VMEM)
    hbm = pl.BlockSpec(memory_space=pl.ANY)
    return pl.pallas_call(
        functools.partial(kernel, ns, nh, rows, dim, width, heads, states, tile, chunk),
        out_shape=jax.ShapeDtypeStruct((span, width), BF16),
        in_specs=[hbm, hbm, hbm, vmem, vmem, vmem, vmem],
        out_specs=vmem,
        scratch_shapes=[
            pltpu.VMEM((GROUP * span, dim), BF16),
            pltpu.VMEM((dim, width), BF16),
            pltpu.VMEM((dim, 4 * states), BF16),
            pltpu.VMEM((span, width), BF16),
            pltpu.VMEM((GROUP, states, width), F32),
            pltpu.VMEM((GROUP, states, width), F32),
            pltpu.VMEM((GROUP, 8, heads), F32),
            pltpu.VMEM((GROUP, 8, heads), F32),
            pltpu.VMEM((2, span, states), BF16),
            pltpu.VMEM((2, span, heads), F32),
            pltpu.VMEM((span, width), F32),
            pltpu.VMEM((chunks, states, chunk), BF16),
            pltpu.VMEM((chunks, states, chunk), BF16),
            pltpu.VMEM((chunks, states, chunk), BF16),
            pltpu.VMEM((chunks, states, chunk), BF16),
            dma((tiles,)),
            dma,
            dma,
            dma((GROUP - 1,)),
            dma((GROUP - 1,)),
            dma((GROUP * (nh - 1),)),
            dma((GROUP * (nh - 1),)),
            dma((chunks,)),
            dma((chunks,)),
            dma((chunks,)),
            dma((chunks,)),
        ],
        compiler_params=pltpu.CompilerParams(
            collective_id=0, has_side_effects=True, vmem_limit_bytes=56 * 1024 * 1024
        ),
    )(
        hidden_in, w_inner, w_inout, w_step, step_bias,
        decay_rate.reshape(1, heads), skip_gain.reshape(1, heads),
    )


def solution(mesh):
    placed = (
        P(("seq", "head"), None),
        P(None, "head"),
        P(),
        P(None, None, "head"),
        P(None, "head"),
        P("head"),
        P("head"),
    )
    return jax.shard_map(
        functools.partial(shards, mesh.shape["seq"], mesh.shape["head"]),
        mesh=mesh, in_specs=placed, out_specs=P("seq", "head"), check_vma=False,
    )
```

```python
import functools

import jax
import jax.numpy as jnp
from jax import lax
from jax.experimental import pallas as pl
from jax.experimental.pallas import tpu as pltpu
from jax.sharding import PartitionSpec as P

HEADDIM = 64
GROUP = 4
MESH = pl.DeviceIdType.MESH
F32 = jnp.float32
BF16 = jnp.bfloat16
EXACT = lax.Precision.HIGHEST


def bdot(a, b):
    return jnp.dot(a, b, preferred_element_type=F32)


def turned(a, b):
    return lax.dot_general(
        a, b, (((0,), (0,)), ((), ())), precision=EXACT, preferred_element_type=F32
    )


def softplus(x):
    return jnp.maximum(x, 0.0) + jnp.log1p(jnp.exp(-jnp.abs(x)))


def halves(x):
    top = x.astype(BF16).astype(F32)
    return jnp.concatenate([top, x - top], axis=1).astype(BF16)


def kernel(
    ns, nh, rows, dim, width, heads, states, tile, chunk,
    x_ref, w_hbm, wio_hbm, ws_ref, bias_ref, rate_ref, skip_ref, out_ref,
    hid, w_ref, wio_ref, inn, st_f, st_b, tot_f, tot_b, own_out, own_scale, acc,
    widen, lines, cum_line, exc_line, step_line_f, step_line_b,
    snd_f, snd_b, rcv_f, rcv_b,
    w_sem, wio_sem, x_sem, peer_send, peer_recv, sib_send, sib_recv,
    fs_sem, fr_sem, bs_sem, br_sem,
):
    s = lax.axis_index("seq")
    h = lax.axis_index("head")
    span = rows * nh
    place = lax.rem(s, GROUP)
    lap = lax.div(s, GROUP)
    laps = ns // GROUP
    first_seq = s - place
    tiles = width // tile
    chunks = width // chunk

    def partner(d):
        px = lax.rem(lax.rem(place, 2) + lax.rem(d, 2), 2)
        py = lax.rem(lax.div(place, 2) + lax.div(d, 2), 2)
        return py * 2 + px

    def sibling(e):
        return lax.rem(h + e, nh)

    def piece(g, hh):
        return pl.ds(pl.multiple_of((g * nh + hh) * rows, rows), rows)

    def columns(t, size):
        return pl.ds(pl.multiple_of(t * size, size), size)

    def w_copy(t):
        return pltpu.make_async_copy(
            w_hbm.at[:, columns(t, tile)], w_ref.at[:, columns(t, tile)], w_sem.at[t]
        )

    own_copy = pltpu.make_async_copy(x_ref, hid.at[piece(place, h)], x_sem)
    own_copy.start()
    wio_copy = pltpu.make_async_copy(wio_hbm, wio_ref, wio_sem)
    wio_copy.start()
    for t in range(tiles):
        w_copy(jnp.int32(t)).start()

    barrier = pltpu.get_barrier_semaphore()
    for d in range(1, GROUP):
        to = first_seq + partner(jnp.int32(d))
        pl.semaphore_signal(barrier, 1, device_id=(to, h), device_id_type=MESH)
    for e in range(1, nh):
        pl.semaphore_signal(barrier, 1, device_id=(s, sibling(e)), device_id_type=MESH)

    @pl.when(lap > 0)
    def _():
        pl.semaphore_signal(barrier, 1, device_id=(s - GROUP, h), device_id_type=MESH)

    @pl.when(lap < laps - 1)
    def _():
        pl.semaphore_signal(barrier, 1, device_id=(s + GROUP, h), device_id_type=MESH)

    near = jnp.where(lap > 0, 1, 0) + jnp.where(lap < laps - 1, 1, 0)
    pl.semaphore_wait(barrier, GROUP - 1 + nh - 1 + near)

    def peer(d):
        return pltpu.make_async_remote_copy(
            src_ref=x_ref,
            dst_ref=hid.at[piece(place, h)],
            send_sem=peer_send.at[d - 1],
            recv_sem=peer_recv.at[d - 1],
            device_id=(first_seq + partner(d), h),
            device_id_type=MESH,
        )

    def sib(d, e, src):
        return pltpu.make_async_remote_copy(
            src_ref=src,
            dst_ref=hid.at[piece(partner(d), h)],
            send_sem=sib_send.at[d * (nh - 1) + e - 1],
            recv_sem=sib_recv.at[d * (nh - 1) + e - 1],
            device_id=(s, sibling(e)),
            device_id_type=MESH,
        )

    zero = jnp.int32(0)
    for e in range(1, nh):
        sib(zero, e, x_ref).start()
    for d in range(1, GROUP):
        peer(jnp.int32(d)).start()

    @pl.when(lap == 0)
    def _():
        rcv_f[...] = jnp.zeros_like(rcv_f)

    @pl.when(lap == laps - 1)
    def _():
        rcv_b[...] = jnp.zeros_like(rcv_b)

    below = lax.broadcasted_iota(jnp.int32, (span, span), 0)
    right = lax.broadcasted_iota(jnp.int32, (span, span), 1)
    left_half = lax.broadcasted_iota(jnp.int32, (1, 128), 1) < HEADDIM
    lower = below > right
    level = below == right
    rate = rate_ref[...]

    part = lax.rem(lax.broadcasted_iota(jnp.int32, (2 * heads, width), 0), heads) * HEADDIM
    column = lax.broadcasted_iota(jnp.int32, (2 * heads, width), 1)
    widen[...] = jnp.where((column >= part) & (column < part + HEADDIM), 1.0, 0.0).astype(BF16)

    def forward(d):
        peer(d).wait_recv()
        for e in range(1, nh):
            sib(d, e, hid.at[piece(partner(d), h)]).start()

    def block(d, carry):
        g = partner(d)

        @pl.when(d == 0)
        def _():
            own_copy.wait()
            wio_copy.wait()

        for e in range(1, nh):
            sib(d, e, hid.at[piece(g, h)]).wait_recv()

        @pl.when((d > 0) & (d < GROUP - 1))
        def _():
            forward(d + 1)

        here = pl.ds(pl.multiple_of(g * span, span), span)
        xb = hid[here, :]
        maps = bdot(xb, wio_ref[...]).astype(BF16)
        over = (((1,), (1,)), ((), ()))
        step_f = softplus(
            lax.dot_general(xb, ws_ref[0], over, preferred_element_type=F32) + bias_ref[0:1, :]
        )
        step_b = softplus(
            lax.dot_general(xb, ws_ref[1], over, preferred_element_type=F32) + bias_ref[1:2, :]
        )
        log_f = -rate * step_f
        log_b = -rate * step_b
        tri = jnp.where(below >= right, 1.0, 0.0).astype(F32)
        cum_f = jnp.dot(tri, log_f, precision=EXACT, preferred_element_type=F32)
        cum_b = jnp.dot(tri, log_b, precision=EXACT, preferred_element_type=F32)
        exc_b = cum_b - log_b
        last_f = cum_f[span - 1 : span, :]
        last_b = cum_b[span - 1 : span, :]
        tot_f[g] = jnp.broadcast_to(last_f, (8, heads))
        tot_b[g] = jnp.broadcast_to(last_b, (8, heads))
        tail_f = halves(jnp.exp(last_f - cum_f) * step_f)
        tail_b = halves(jnp.exp(exc_b) * step_b)
        in_f = maps[:, :states].astype(F32).T.astype(BF16)
        in_b = maps[:, 2 * states : 3 * states].astype(F32).T.astype(BF16)

        def project(t, carry):
            cols = columns(t, tile)

            @pl.when(d == 0)
            def _():
                w_copy(t).wait()

            values = bdot(hid[here, :], w_ref[:, cols]).astype(BF16)
            inn[:, cols] = values
            wide = values.astype(F32)
            grow = widen[:, cols]
            st_f[g, :, cols] = bdot(in_f, (bdot(tail_f, grow) * wide).astype(BF16))
            st_b[g, :, cols] = bdot(in_b, (bdot(tail_b, grow) * wide).astype(BF16))
            return carry

        lax.fori_loop(0, tiles, project, 0)

        @pl.when(d == 0)
        def _():
            forward(d + 1)
            out_f = maps[:, states : 2 * states]
            out_b = maps[:, 3 * states :]
            own_out[0] = out_f
            own_out[1] = out_b
            own_scale[0] = halves(jnp.exp(cum_f))
            own_scale[1] = halves(jnp.exp(last_b - exc_b))
            score = jnp.where(
                lower,
                lax.dot_general(out_f, maps[:, :states], over, preferred_element_type=F32),
                lax.dot_general(
                    out_b, maps[:, 2 * states : 3 * states], over, preferred_element_type=F32
                ),
            )
            score = jnp.where(level, 0.0, score)
            unit = jnp.where(level, 1.0, 0.0).astype(F32)
            cum_line[...] = turned(cum_f, unit)
            exc_line[...] = turned(exc_b, unit)
            step_line_f[...] = turned(step_f, unit)
            step_line_b[...] = turned(step_b, unit)
            cum_two = halves(cum_f)
            exc_two = halves(exc_b)
            skip_two = halves(jnp.broadcast_to(skip_ref[...], (8, heads)))
            owner = lax.rem(lax.broadcasted_iota(jnp.int32, (2 * heads, 128), 0), heads)

            def mix(i, carry):
                cols = columns(i, 128)
                both = inn[:, cols]
                parts = []
                for k in (2 * i, 2 * i + 1):
                    pick = jnp.where(owner == k, 1.0, 0.0).astype(BF16)
                    one = pl.ds(k, 1)
                    gap = jnp.where(
                        lower,
                        bdot(cum_two, pick) - cum_line[one, :],
                        exc_line[one, :] - bdot(exc_two, pick),
                    )
                    scale = jnp.where(lower, step_line_f[one, :], step_line_b[one, :])
                    parts.append(bdot((jnp.exp(gap) * (score * scale)).astype(BF16), both))
                gain = bdot(skip_two, widen[:, cols])[0:1, :]
                acc[:, cols] = jnp.where(left_half, parts[0], parts[1]) + gain * both.astype(F32)
                return carry

            lax.fori_loop(0, heads // 2, mix, 0)

        return carry

    lax.fori_loop(0, GROUP, block, 0)

    tf = [tot_f[b][0:1, :] for b in range(GROUP)]
    tb = [tot_b[b][0:1, :] for b in range(GROUP)]
    none = jnp.zeros_like(tf[0])

    def between(logs, keep):
        return jnp.exp(sum([jnp.where(keep(b), logs[b], none) for b in range(GROUP)], none))

    all_f = [between(tf, lambda c, b=b: jnp.asarray(c > b)) for b in range(GROUP)]
    all_b = [between(tb, lambda c, b=b: jnp.asarray(c < b)) for b in range(GROUP)]
    whole_f = between(tf, lambda c: jnp.asarray(True))
    whole_b = between(tb, lambda c: jnp.asarray(True))
    mine_f = [
        jnp.where(b < place, between(tf, lambda c, b=b: (c > b) & (c < place)), none)
        for b in range(GROUP)
    ]
    mine_b = [
        jnp.where(b > place, between(tb, lambda c, b=b: (c < b) & (c > place)), none)
        for b in range(GROUP)
    ]
    reach_f = between(tf, lambda c: c < place)
    reach_b = between(tb, lambda c: c > place)
    every = all_f + [whole_f] + mine_f + [reach_f] + all_b + [whole_b] + mine_b + [reach_b]
    every = every + [none] * (-len(every) % 8)
    lines[...] = bdot(halves(jnp.concatenate(every, axis=0)), widen[...])

    def f_copy(k):
        return pltpu.make_async_remote_copy(
            src_ref=snd_f.at[k], dst_ref=rcv_f.at[k], send_sem=fs_sem.at[k], recv_sem=fr_sem.at[k],
            device_id=(s + GROUP, h), device_id_type=MESH,
        )

    def b_copy(k):
        return pltpu.make_async_remote_copy(
            src_ref=snd_b.at[k], dst_ref=rcv_b.at[k], send_sem=bs_sem.at[k], recv_sem=br_sem.at[k],
            device_id=(s - GROUP, h), device_id_type=MESH,
        )

    def step(k, base, st, rcv, snd, copy, got, sent):
        cols = columns(k, chunk)
        line = lines[:, cols]

        def gathered(first):
            total = line[first + GROUP : first + GROUP + 1] * rcv[k].astype(F32)
            for b in range(GROUP):
                total = total + line[first + b : first + b + 1] * st[b, :, cols]
            return total.astype(BF16)

        @pl.when(got)
        def _():
            copy(k).wait_recv()

        @pl.when(sent)
        def _():
            snd[k] = gathered(base)
            copy(k).start()

        return gathered(base + GROUP + 1)

    def finish(k, carry):
        cols = columns(k, chunk)
        ahead = step(k, 0, st_f, rcv_f, snd_f, f_copy, lap > 0, lap < laps - 1)
        behind = step(
            k, 2 * GROUP + 2, st_b, rcv_b, snd_b, b_copy, lap < laps - 1, lap > 0
        )
        grow = widen[:, cols]
        result = acc[:, cols] + bdot(own_scale[0], grow) * bdot(own_out[0], ahead)
        result = result + bdot(own_scale[1], grow) * bdot(own_out[1], behind)
        out_ref[:, cols] = result.astype(out_ref.dtype)
        return carry

    lax.fori_loop(0, chunks, finish, 0)

    for d in range(1, GROUP):
        peer(jnp.int32(d)).wait_send()
    for d in range(GROUP):
        for e in range(1, nh):
            sib(jnp.int32(d), e, x_ref).wait_send()

    @pl.when(lap < laps - 1)
    def _():
        lax.fori_loop(0, chunks, lambda k, c: (f_copy(k).wait_send(), c)[1], 0)

    @pl.when(lap > 0)
    def _():
        lax.fori_loop(0, chunks, lambda k, c: (b_copy(k).wait_send(), c)[1], 0)


def shards(ns, nh, hidden_in, w_inner, w_inout, w_step, step_bias, decay_rate, skip_gain):
    rows, dim = hidden_in.shape
    width = w_inner.shape[1]
    heads = w_step.shape[2]
    states = w_inout.shape[1] // 4
    span = rows * nh
    tile = 512
    chunk = 256
    tiles, chunks = width // tile, width // chunk
    dma = pltpu.SemaphoreType.DMA
    vmem = pl.BlockSpec(memory_space=pltpu.VMEM)
    hbm = pl.BlockSpec(memory_space=pl.ANY)
    return pl.pallas_call(
        functools.partial(kernel, ns, nh, rows, dim, width, heads, states, tile, chunk),
        out_shape=jax.ShapeDtypeStruct((span, width), BF16),
        in_specs=[hbm, hbm, hbm, vmem, vmem, vmem, vmem],
        out_specs=vmem,
        scratch_shapes=[
            pltpu.VMEM((GROUP * span, dim), BF16),
            pltpu.VMEM((dim, width), BF16),
            pltpu.VMEM((dim, 4 * states), BF16),
            pltpu.VMEM((span, width), BF16),
            pltpu.VMEM((GROUP, states, width), F32),
            pltpu.VMEM((GROUP, states, width), F32),
            pltpu.VMEM((GROUP, 8, heads), F32),
            pltpu.VMEM((GROUP, 8, heads), F32),
            pltpu.VMEM((2, span, states), BF16),
            pltpu.VMEM((2, span, 2 * heads), BF16),
            pltpu.VMEM((span, width), F32),
            pltpu.VMEM((2 * heads, width), BF16),
            pltpu.VMEM((24, width), F32),
            pltpu.VMEM((heads, span), F32),
            pltpu.VMEM((heads, span), F32),
            pltpu.VMEM((heads, span), F32),
            pltpu.VMEM((heads, span), F32),
            pltpu.VMEM((chunks, states, chunk), BF16),
            pltpu.VMEM((chunks, states, chunk), BF16),
            pltpu.VMEM((chunks, states, chunk), BF16),
            pltpu.VMEM((chunks, states, chunk), BF16),
            dma((tiles,)),
            dma,
            dma,
            dma((GROUP - 1,)),
            dma((GROUP - 1,)),
            dma((GROUP * (nh - 1),)),
            dma((GROUP * (nh - 1),)),
            dma((chunks,)),
            dma((chunks,)),
            dma((chunks,)),
            dma((chunks,)),
        ],
        compiler_params=pltpu.CompilerParams(
            collective_id=0, has_side_effects=True, vmem_limit_bytes=56 * 1024 * 1024
        ),
    )(
        hidden_in, w_inner, w_inout, jnp.swapaxes(w_step, 1, 2), step_bias,
        decay_rate.reshape(1, heads), skip_gain.reshape(1, heads),
    )


def solution(mesh):
    placed = (
        P(("seq", "head"), None),
        P(None, "head"),
        P(),
        P(None, None, "head"),
        P(None, "head"),
        P("head"),
        P("head"),
    )
    return jax.shard_map(
        functools.partial(shards, mesh.shape["seq"], mesh.shape["head"]),
        mesh=mesh, in_specs=placed, out_specs=P("seq", "head"), check_vma=False,
    )
```

```python
import functools

import jax
import jax.numpy as jnp
from jax import lax
from jax.experimental import pallas as pl
from jax.experimental.pallas import tpu as pltpu
from jax.sharding import PartitionSpec as P

HEADDIM = 64
GROUP = 4
MESH = pl.DeviceIdType.MESH
F32 = jnp.float32
BF16 = jnp.bfloat16
EXACT = lax.Precision.HIGHEST


def bdot(a, b):
    return jnp.dot(a, b, preferred_element_type=F32)


def turned(a, b):
    return lax.dot_general(
        a, b, (((0,), (0,)), ((), ())), precision=EXACT, preferred_element_type=F32
    )


def softplus(x):
    return jnp.maximum(x, 0.0) + jnp.log1p(jnp.exp(-jnp.abs(x)))


def halves(x):
    top = x.astype(BF16).astype(F32)
    return jnp.concatenate([top, x - top], axis=1).astype(BF16)


def kernel(
    ns, nh, rows, dim, width, heads, states, tile, chunk,
    x_ref, w_hbm, wio_hbm, ws_ref, bias_ref, rate_ref, skip_ref, out_ref,
    hid, w_ref, wio_ref, inn, st_f, st_b, tot_f, tot_b, own_out, own_scale, acc,
    widen, lines, cum_line, exc_line, step_line_f, step_line_b,
    snd_f, snd_b, rcv_f, rcv_b,
    w_sem, wio_sem, x_sem, peer_send, peer_recv, sib_send, sib_recv,
    fs_sem, fr_sem, bs_sem, br_sem,
):
    s = lax.axis_index("seq")
    h = lax.axis_index("head")
    span = rows * nh
    place = lax.rem(s, GROUP)
    lap = lax.div(s, GROUP)
    laps = ns // GROUP
    first_seq = s - place
    tiles = width // tile
    chunks = width // chunk

    def partner(d):
        px = lax.rem(lax.rem(place, 2) + lax.rem(d, 2), 2)
        py = lax.rem(lax.div(place, 2) + lax.div(d, 2), 2)
        return py * 2 + px

    def sibling(e):
        return lax.rem(h + e, nh)

    def piece(g, hh):
        return pl.ds(pl.multiple_of((g * nh + hh) * rows, rows), rows)

    def columns(t, size):
        return pl.ds(pl.multiple_of(t * size, size), size)

    def w_copy(t):
        return pltpu.make_async_copy(
            w_hbm.at[:, columns(t, tile)], w_ref.at[:, columns(t, tile)], w_sem.at[t]
        )

    own_copy = pltpu.make_async_copy(x_ref, hid.at[piece(place, h)], x_sem)
    own_copy.start()
    wio_copy = pltpu.make_async_copy(wio_hbm, wio_ref, wio_sem)
    wio_copy.start()
    for t in range(tiles):
        w_copy(jnp.int32(t)).start()

    barrier = pltpu.get_barrier_semaphore()
    for d in range(1, GROUP):
        to = first_seq + partner(jnp.int32(d))
        pl.semaphore_signal(barrier, 1, device_id=(to, h), device_id_type=MESH)
    for e in range(1, nh):
        pl.semaphore_signal(barrier, 1, device_id=(s, sibling(e)), device_id_type=MESH)

    @pl.when(lap > 0)
    def _():
        pl.semaphore_signal(barrier, 1, device_id=(s - GROUP, h), device_id_type=MESH)

    @pl.when(lap < laps - 1)
    def _():
        pl.semaphore_signal(barrier, 1, device_id=(s + GROUP, h), device_id_type=MESH)

    near = jnp.where(lap > 0, 1, 0) + jnp.where(lap < laps - 1, 1, 0)
    pl.semaphore_wait(barrier, GROUP - 1 + nh - 1 + near)

    def peer(d):
        return pltpu.make_async_remote_copy(
            src_ref=x_ref,
            dst_ref=hid.at[piece(place, h)],
            send_sem=peer_send.at[d - 1],
            recv_sem=peer_recv.at[d - 1],
            device_id=(first_seq + partner(d), h),
            device_id_type=MESH,
        )

    def sib(d, e, src):
        return pltpu.make_async_remote_copy(
            src_ref=src,
            dst_ref=hid.at[piece(partner(d), h)],
            send_sem=sib_send.at[d * (nh - 1) + e - 1],
            recv_sem=sib_recv.at[d * (nh - 1) + e - 1],
            device_id=(s, sibling(e)),
            device_id_type=MESH,
        )

    zero = jnp.int32(0)
    for e in range(1, nh):
        sib(zero, e, x_ref).start()
    for d in range(1, GROUP):
        peer(jnp.int32(d)).start()

    @pl.when(lap == 0)
    def _():
        rcv_f[...] = jnp.zeros_like(rcv_f)

    @pl.when(lap == laps - 1)
    def _():
        rcv_b[...] = jnp.zeros_like(rcv_b)

    below = lax.broadcasted_iota(jnp.int32, (span, span), 0)
    right = lax.broadcasted_iota(jnp.int32, (span, span), 1)
    left_half = lax.broadcasted_iota(jnp.int32, (1, 128), 1) < HEADDIM
    lower = below > right
    level = below == right
    rate = rate_ref[...]

    part = lax.rem(lax.broadcasted_iota(jnp.int32, (2 * heads, width), 0), heads) * HEADDIM
    column = lax.broadcasted_iota(jnp.int32, (2 * heads, width), 1)
    widen[...] = jnp.where((column >= part) & (column < part + HEADDIM), 1.0, 0.0).astype(BF16)

    def forward(d):
        peer(d).wait_recv()
        for e in range(1, nh):
            sib(d, e, hid.at[piece(partner(d), h)]).start()

    def block(d, carry):
        g = partner(d)

        @pl.when(d == 0)
        def _():
            own_copy.wait()
            wio_copy.wait()

        for e in range(1, nh):
            sib(d, e, hid.at[piece(g, h)]).wait_recv()

        @pl.when((d > 0) & (d < GROUP - 1))
        def _():
            forward(d + 1)

        here = pl.ds(pl.multiple_of(g * span, span), span)
        xb = hid[here, :]
        maps = bdot(xb, wio_ref[...]).astype(BF16)
        over = (((1,), (1,)), ((), ()))
        step_f = softplus(
            lax.dot_general(xb, ws_ref[0], over, preferred_element_type=F32) + bias_ref[0:1, :]
        )
        step_b = softplus(
            lax.dot_general(xb, ws_ref[1], over, preferred_element_type=F32) + bias_ref[1:2, :]
        )
        log_f = -rate * step_f
        log_b = -rate * step_b
        tri = jnp.where(below >= right, 1.0, 0.0).astype(F32)
        cum_f = jnp.dot(tri, log_f, precision=EXACT, preferred_element_type=F32)
        cum_b = jnp.dot(tri, log_b, precision=EXACT, preferred_element_type=F32)
        exc_b = cum_b - log_b
        last_f = cum_f[span - 1 : span, :]
        last_b = cum_b[span - 1 : span, :]
        tot_f[g] = jnp.broadcast_to(last_f, (8, heads))
        tot_b[g] = jnp.broadcast_to(last_b, (8, heads))
        tail_f = halves(jnp.exp(last_f - cum_f) * step_f)
        tail_b = halves(jnp.exp(exc_b) * step_b)
        in_f = maps[:, :states].astype(F32).T.astype(BF16)
        in_b = maps[:, 2 * states : 3 * states].astype(F32).T.astype(BF16)

        def project(t, carry):
            cols = columns(t, tile)

            @pl.when(d == 0)
            def _():
                w_copy(t).wait()

            values = bdot(hid[here, :], w_ref[:, cols]).astype(BF16)
            inn[:, cols] = values
            wide = values.astype(F32)
            grow = widen[:, cols]
            st_f[g, :, cols] = bdot(in_f, (bdot(tail_f, grow) * wide).astype(BF16))
            st_b[g, :, cols] = bdot(in_b, (bdot(tail_b, grow) * wide).astype(BF16))
            return carry

        lax.fori_loop(0, tiles, project, 0)

        @pl.when(d == 0)
        def _():
            forward(d + 1)
            out_f = maps[:, states : 2 * states]
            out_b = maps[:, 3 * states :]
            own_out[0] = out_f
            own_out[1] = out_b
            own_scale[0] = halves(jnp.exp(cum_f))
            own_scale[1] = halves(jnp.exp(last_b - exc_b))
            score = jnp.where(
                lower,
                lax.dot_general(out_f, maps[:, :states], over, preferred_element_type=F32),
                lax.dot_general(
                    out_b, maps[:, 2 * states : 3 * states], over, preferred_element_type=F32
                ),
            )
            score = jnp.where(level, 0.0, score)
            unit = jnp.where(level, 1.0, 0.0).astype(F32)
            cum_line[...] = turned(cum_f, unit)
            exc_line[...] = turned(exc_b, unit)
            step_line_f[...] = turned(step_f, unit)
            step_line_b[...] = turned(step_b, unit)
            cum_two = halves(cum_f)
            exc_two = halves(exc_b)
            skip_two = halves(jnp.broadcast_to(skip_ref[...], (8, heads)))
            owner = lax.rem(lax.broadcasted_iota(jnp.int32, (2 * heads, 128), 0), heads)

            def mix(i, carry):
                cols = columns(i, 128)
                both = inn[:, cols]
                parts = []
                for k in (2 * i, 2 * i + 1):
                    pick = jnp.where(owner == k, 1.0, 0.0).astype(BF16)
                    one = pl.ds(k, 1)
                    gap = jnp.where(
                        lower,
                        bdot(cum_two, pick) - cum_line[one, :],
                        exc_line[one, :] - bdot(exc_two, pick),
                    )
                    scale = jnp.where(lower, step_line_f[one, :], step_line_b[one, :])
                    parts.append(bdot((jnp.exp(gap) * (score * scale)).astype(BF16), both))
                gain = bdot(skip_two, widen[:, cols])[0:1, :]
                acc[:, cols] = jnp.where(left_half, parts[0], parts[1]) + gain * both.astype(F32)
                return carry

            lax.fori_loop(0, heads // 2, mix, 0)

        return carry

    lax.fori_loop(0, GROUP, block, 0)

    tf = [tot_f[b][0:1, :] for b in range(GROUP)]
    tb = [tot_b[b][0:1, :] for b in range(GROUP)]
    none = jnp.zeros_like(tf[0])

    def between(logs, keep):
        return jnp.exp(sum([jnp.where(keep(b), logs[b], none) for b in range(GROUP)], none))

    all_f = [between(tf, lambda c, b=b: jnp.asarray(c > b)) for b in range(GROUP)]
    all_b = [between(tb, lambda c, b=b: jnp.asarray(c < b)) for b in range(GROUP)]
    whole_f = between(tf, lambda c: jnp.asarray(True))
    whole_b = between(tb, lambda c: jnp.asarray(True))
    mine_f = [
        jnp.where(b < place, between(tf, lambda c, b=b: (c > b) & (c < place)), none)
        for b in range(GROUP)
    ]
    mine_b = [
        jnp.where(b > place, between(tb, lambda c, b=b: (c < b) & (c > place)), none)
        for b in range(GROUP)
    ]
    reach_f = between(tf, lambda c: c < place)
    reach_b = between(tb, lambda c: c > place)
    every = all_f + [whole_f] + mine_f + [reach_f] + all_b + [whole_b] + mine_b + [reach_b]
    every = every + [none] * (-len(every) % 8)
    lines[...] = bdot(halves(jnp.concatenate(every, axis=0)), widen[...])

    def f_copy(k):
        return pltpu.make_async_remote_copy(
            src_ref=snd_f.at[k], dst_ref=rcv_f.at[k], send_sem=fs_sem.at[k], recv_sem=fr_sem.at[k],
            device_id=(s + GROUP, h), device_id_type=MESH,
        )

    def b_copy(k):
        return pltpu.make_async_remote_copy(
            src_ref=snd_b.at[k], dst_ref=rcv_b.at[k], send_sem=bs_sem.at[k], recv_sem=br_sem.at[k],
            device_id=(s - GROUP, h), device_id_type=MESH,
        )

    def gathered(k, first, st, rcv):
        cols = columns(k, chunk)
        line = lines[:, cols]
        total = line[first + GROUP : first + GROUP + 1] * rcv[k].astype(F32)
        for b in range(GROUP):
            total = total + line[first + b : first + b + 1] * st[b, :, cols]
        return total.astype(BF16)

    def pass_on(k, base, st, rcv, snd, copy, got, sent):
        inside = (k >= 0) & (k < chunks)

        @pl.when(inside & got)
        def _():
            copy(k).wait_recv()

        @pl.when(inside & sent)
        def _():
            snd[k] = gathered(k, base, st, rcv)
            copy(k).start()

    lag_f = lap
    lag_b = laps - 1 - lap
    lag = jnp.maximum(lag_f, lag_b)

    def slot(n, carry):
        pass_on(n - lag_f, 0, st_f, rcv_f, snd_f, f_copy, lap > 0, lap < laps - 1)
        pass_on(
            n - lag_b, 2 * GROUP + 2, st_b, rcv_b, snd_b, b_copy, lap < laps - 1, lap > 0
        )
        k = n - lag

        @pl.when((k >= 0) & (k < chunks))
        def _():
            cols = columns(k, chunk)
            ahead = gathered(k, GROUP + 1, st_f, rcv_f)
            behind = gathered(k, 3 * GROUP + 3, st_b, rcv_b)
            grow = widen[:, cols]
            result = acc[:, cols] + bdot(own_scale[0], grow) * bdot(own_out[0], ahead)
            result = result + bdot(own_scale[1], grow) * bdot(own_out[1], behind)
            out_ref[:, cols] = result.astype(out_ref.dtype)

        return carry

    lax.fori_loop(0, chunks + laps - 1, slot, 0)

    for d in range(1, GROUP):
        peer(jnp.int32(d)).wait_send()
    for d in range(GROUP):
        for e in range(1, nh):
            sib(jnp.int32(d), e, x_ref).wait_send()

    @pl.when(lap < laps - 1)
    def _():
        lax.fori_loop(0, chunks, lambda k, c: (f_copy(k).wait_send(), c)[1], 0)

    @pl.when(lap > 0)
    def _():
        lax.fori_loop(0, chunks, lambda k, c: (b_copy(k).wait_send(), c)[1], 0)


def shards(ns, nh, hidden_in, w_inner, w_inout, w_step, step_bias, decay_rate, skip_gain):
    rows, dim = hidden_in.shape
    width = w_inner.shape[1]
    heads = w_step.shape[2]
    states = w_inout.shape[1] // 4
    span = rows * nh
    tile = 512
    chunk = 256
    tiles, chunks = width // tile, width // chunk
    dma = pltpu.SemaphoreType.DMA
    vmem = pl.BlockSpec(memory_space=pltpu.VMEM)
    hbm = pl.BlockSpec(memory_space=pl.ANY)
    return pl.pallas_call(
        functools.partial(kernel, ns, nh, rows, dim, width, heads, states, tile, chunk),
        out_shape=jax.ShapeDtypeStruct((span, width), BF16),
        in_specs=[hbm, hbm, hbm, vmem, vmem, vmem, vmem],
        out_specs=vmem,
        scratch_shapes=[
            pltpu.VMEM((GROUP * span, dim), BF16),
            pltpu.VMEM((dim, width), BF16),
            pltpu.VMEM((dim, 4 * states), BF16),
            pltpu.VMEM((span, width), BF16),
            pltpu.VMEM((GROUP, states, width), F32),
            pltpu.VMEM((GROUP, states, width), F32),
            pltpu.VMEM((GROUP, 8, heads), F32),
            pltpu.VMEM((GROUP, 8, heads), F32),
            pltpu.VMEM((2, span, states), BF16),
            pltpu.VMEM((2, span, 2 * heads), BF16),
            pltpu.VMEM((span, width), F32),
            pltpu.VMEM((2 * heads, width), BF16),
            pltpu.VMEM((24, width), F32),
            pltpu.VMEM((heads, span), F32),
            pltpu.VMEM((heads, span), F32),
            pltpu.VMEM((heads, span), F32),
            pltpu.VMEM((heads, span), F32),
            pltpu.VMEM((chunks, states, chunk), BF16),
            pltpu.VMEM((chunks, states, chunk), BF16),
            pltpu.VMEM((chunks, states, chunk), BF16),
            pltpu.VMEM((chunks, states, chunk), BF16),
            dma((tiles,)),
            dma,
            dma,
            dma((GROUP - 1,)),
            dma((GROUP - 1,)),
            dma((GROUP * (nh - 1),)),
            dma((GROUP * (nh - 1),)),
            dma((chunks,)),
            dma((chunks,)),
            dma((chunks,)),
            dma((chunks,)),
        ],
        compiler_params=pltpu.CompilerParams(
            collective_id=0, has_side_effects=True, vmem_limit_bytes=56 * 1024 * 1024
        ),
    )(
        hidden_in, w_inner, w_inout, jnp.swapaxes(w_step, 1, 2), step_bias,
        decay_rate.reshape(1, heads), skip_gain.reshape(1, heads),
    )


def solution(mesh):
    placed = (
        P(("seq", "head"), None),
        P(None, "head"),
        P(),
        P(None, None, "head"),
        P(None, "head"),
        P("head"),
        P("head"),
    )
    return jax.shard_map(
        functools.partial(shards, mesh.shape["seq"], mesh.shape["head"]),
        mesh=mesh, in_specs=placed, out_specs=P("seq", "head"), check_vma=False,
    )
```

```python
import functools

import jax
import jax.numpy as jnp
from jax import lax
from jax.experimental import pallas as pl
from jax.experimental.pallas import tpu as pltpu
from jax.sharding import PartitionSpec as P

HEADDIM = 64
GROUP = 4
MESH = pl.DeviceIdType.MESH
F32 = jnp.float32
BF16 = jnp.bfloat16
EXACT = lax.Precision.HIGHEST


def bdot(a, b):
    return jnp.dot(a, b, preferred_element_type=F32)


def turned(a, b):
    return lax.dot_general(
        a, b, (((0,), (0,)), ((), ())), precision=EXACT, preferred_element_type=F32
    )


def softplus(x):
    return jnp.maximum(x, 0.0) + jnp.log1p(jnp.exp(-jnp.abs(x)))


def halves(x):
    top = x.astype(BF16).astype(F32)
    return jnp.concatenate([top, x - top], axis=1).astype(BF16)


def kernel(
    ns, nh, rows, dim, width, heads, states, tile, chunk,
    x_ref, w_hbm, wio_hbm, ws_ref, bias_ref, rate_ref, skip_ref, out_ref,
    hid, w_ref, wio_ref, inn, st_f, st_b, own_out, own_scale, acc,
    widen_f, widen_b, lines, cum_line, exc_line, step_line, tails, in_turn,
    snd_f, snd_b, rcv_f, rcv_b,
    w_sem, wio_sem, x_sem, peer_send, peer_recv, sib_send, sib_recv,
    fs_sem, fr_sem, bs_sem, br_sem,
):
    s = lax.axis_index("seq")
    h = lax.axis_index("head")
    span = rows * nh
    place = lax.rem(s, GROUP)
    lap = lax.div(s, GROUP)
    laps = ns // GROUP
    first_seq = s - place
    tiles = width // tile
    chunks = width // chunk

    def partner(d):
        px = lax.rem(lax.rem(place, 2) + lax.rem(d, 2), 2)
        py = lax.rem(lax.div(place, 2) + lax.div(d, 2), 2)
        return py * 2 + px

    def sibling(e):
        return lax.rem(h + e, nh)

    def piece(d, hh):
        return pl.ds(pl.multiple_of((d * nh + hh) * rows, rows), rows)

    def columns(t, size):
        return pl.ds(pl.multiple_of(t * size, size), size)

    def w_copy(t):
        return pltpu.make_async_copy(
            w_hbm.at[:, columns(t, tile)], w_ref.at[:, columns(t, tile)], w_sem.at[t]
        )

    own_copy = pltpu.make_async_copy(x_ref, hid.at[piece(0, h)], x_sem)
    own_copy.start()
    wio_copy = pltpu.make_async_copy(wio_hbm, wio_ref, wio_sem)
    wio_copy.start()
    for t in range(tiles):
        w_copy(jnp.int32(t)).start()

    barrier = pltpu.get_barrier_semaphore()
    for d in range(1, GROUP):
        to = first_seq + partner(jnp.int32(d))
        pl.semaphore_signal(barrier, 1, device_id=(to, h), device_id_type=MESH)
    for e in range(1, nh):
        pl.semaphore_signal(barrier, 1, device_id=(s, sibling(e)), device_id_type=MESH)

    @pl.when(lap > 0)
    def _():
        pl.semaphore_signal(barrier, 1, device_id=(s - GROUP, h), device_id_type=MESH)

    @pl.when(lap < laps - 1)
    def _():
        pl.semaphore_signal(barrier, 1, device_id=(s + GROUP, h), device_id_type=MESH)

    near = jnp.where(lap > 0, 1, 0) + jnp.where(lap < laps - 1, 1, 0)
    pl.semaphore_wait(barrier, GROUP - 1 + nh - 1 + near)

    def peer(d):
        return pltpu.make_async_remote_copy(
            src_ref=x_ref,
            dst_ref=hid.at[piece(d, h)],
            send_sem=peer_send.at[d - 1],
            recv_sem=peer_recv.at[d - 1],
            device_id=(first_seq + partner(d), h),
            device_id_type=MESH,
        )

    def sib(d, e, src):
        return pltpu.make_async_remote_copy(
            src_ref=src,
            dst_ref=hid.at[piece(d, h)],
            send_sem=sib_send.at[d * (nh - 1) + e - 1],
            recv_sem=sib_recv.at[d * (nh - 1) + e - 1],
            device_id=(s, sibling(e)),
            device_id_type=MESH,
        )

    zero = jnp.int32(0)
    for e in range(1, nh):
        sib(zero, e, x_ref).start()
    for d in range(1, GROUP):
        peer(jnp.int32(d)).start()

    @pl.when(lap == 0)
    def _():
        rcv_f[...] = jnp.zeros_like(rcv_f)

    @pl.when(lap == laps - 1)
    def _():
        rcv_b[...] = jnp.zeros_like(rcv_b)

    below = lax.broadcasted_iota(jnp.int32, (span, span), 0)
    right = lax.broadcasted_iota(jnp.int32, (span, span), 1)
    left_half = lax.broadcasted_iota(jnp.int32, (1, 128), 1) < HEADDIM
    lower = below > right
    level = below == right
    tri = jnp.where(below >= right, 1.0, 0.0).astype(F32)
    over = (((1,), (1,)), ((), ()))
    rate = jnp.concatenate([rate_ref[...], rate_ref[...]], axis=1)
    bias = jnp.concatenate([bias_ref[0:1, :], bias_ref[1:2, :]], axis=1)
    two = 2 * heads
    is_fwd = lax.broadcasted_iota(jnp.int32, (span, two), 1) < heads

    part = lax.rem(lax.broadcasted_iota(jnp.int32, (2 * two, width), 0), two) * HEADDIM
    column = lax.broadcasted_iota(jnp.int32, (2 * two, width), 1)
    widen_f[...] = jnp.where((column >= part) & (column < part + HEADDIM), 1.0, 0.0).astype(BF16)
    part = part - width
    widen_b[...] = jnp.where((column >= part) & (column < part + HEADDIM), 1.0, 0.0).astype(BF16)

    def forward(d):
        peer(d).wait_recv()
        for e in range(1, nh):
            sib(d, e, hid.at[piece(d, h)]).start()

    def prepare(xb):
        maps = bdot(xb, wio_ref[...]).astype(BF16)
        steps = softplus(
            lax.dot_general(xb, ws_ref[...], over, preferred_element_type=F32) + bias
        )
        return maps, steps, -rate * steps

    def sums(steps, logs):
        cum = jnp.dot(tri, logs, precision=EXACT, preferred_element_type=F32)
        exc = cum - logs
        last = cum[span - 1 : span, :]
        tail = jnp.exp(jnp.where(is_fwd, last - cum, exc)) * steps
        return cum, exc, last, halves(tail)

    def turn(m):
        return m.astype(F32).T.astype(BF16)

    own_copy.wait()
    for e in range(1, nh):
        sib(zero, e, x_ref).wait_recv()
    wio_copy.wait()
    maps, steps, logs = prepare(hid[0:span, :])
    cum, exc, last_own, tail_own = sums(steps, logs)
    in_f = turn(maps[:, :states])
    in_b = turn(maps[:, 2 * states : 3 * states])

    def project_own(t, carry):
        cols = columns(t, tile)
        w_copy(t).wait()
        values = bdot(hid[0:span, :], w_ref[:, cols]).astype(BF16)
        inn[:, cols] = values
        wide = values.astype(F32)
        st_f[0, :, cols] = bdot(in_f, (bdot(tail_own, widen_f[:, cols]) * wide).astype(BF16))
        st_b[0, :, cols] = bdot(in_b, (bdot(tail_own, widen_b[:, cols]) * wide).astype(BF16))
        return carry

    lax.fori_loop(0, tiles, project_own, 0)
    forward(jnp.int32(1))

    out_f = maps[:, states : 2 * states]
    out_b = maps[:, 3 * states :]
    own_out[0] = out_f
    own_out[1] = out_b
    own_scale[...] = halves(jnp.exp(jnp.where(is_fwd, cum, last_own - exc)))
    score = jnp.where(
        lower,
        lax.dot_general(out_f, maps[:, :states], over, preferred_element_type=F32),
        lax.dot_general(
            out_b, maps[:, 2 * states : 3 * states], over, preferred_element_type=F32
        ),
    )
    score = jnp.where(level, 0.0, score)
    unit = jnp.where(level, 1.0, 0.0).astype(F32)
    cum_line[...] = turned(cum, unit)
    exc_line[...] = turned(exc, unit)
    step_line[...] = turned(steps, unit)
    cum_two = halves(cum)
    exc_two = halves(exc)
    skip_two = halves(
        jnp.broadcast_to(jnp.concatenate([skip_ref[...], skip_ref[...]], axis=1), (8, two))
    )
    owner = lax.rem(lax.broadcasted_iota(jnp.int32, (2 * two, 128), 0), two)

    def mix(i, carry):
        cols = columns(i, 128)
        both = inn[:, cols]
        parts = []
        for k in (2 * i, 2 * i + 1):
            pick_f = jnp.where(owner == k, 1.0, 0.0).astype(BF16)
            pick_b = jnp.where(owner == k + heads, 1.0, 0.0).astype(BF16)
            fwd = pl.ds(k, 1)
            bwd = pl.ds(k + heads, 1)
            gap = jnp.where(
                lower,
                bdot(cum_two, pick_f) - cum_line[fwd, :],
                exc_line[bwd, :] - bdot(exc_two, pick_b),
            )
            scale = jnp.where(lower, step_line[fwd, :], step_line[bwd, :])
            parts.append(bdot((jnp.exp(gap) * (score * scale)).astype(BF16), both))
        gain = bdot(skip_two, widen_f[:, cols])[0:1, :]
        acc[:, cols] = jnp.where(left_half, parts[0], parts[1]) + gain * both.astype(F32)
        return carry

    lax.fori_loop(0, heads // 2, mix, 0)

    for d in range(2, GROUP):
        forward(jnp.int32(d))
    for d in range(1, GROUP):
        for e in range(1, nh):
            sib(jnp.int32(d), e, x_ref).wait_recv()
    maps, steps, logs = prepare(hid[span:, :])
    lasts = [last_own]
    for d in range(1, GROUP):
        mine = slice((d - 1) * span, d * span)
        _, _, last, tail = sums(steps[mine], logs[mine])
        lasts.append(last)
        tails[mine, :] = tail
        in_turn[0, d - 1] = turn(maps[mine, :states])
        in_turn[1, d - 1] = turn(maps[mine, 2 * states : 3 * states])

    def project(k):
        cols = columns(k, chunk)
        wide = bdot(hid[span:, :], w_ref[:, cols]).astype(BF16).astype(F32)
        for way, grow, st in ((0, widen_f, st_f), (1, widen_b, st_b)):
            scaled = (bdot(tails[...], grow[:, cols]) * wide).astype(BF16)
            for d in range(1, GROUP):
                st[d, :, cols] = bdot(in_turn[way, d - 1], scaled[(d - 1) * span : d * span])

    at = [partner(jnp.int32(d)) for d in range(GROUP)]
    none = jnp.zeros_like(last_own)

    def between(keep):
        kept = [jnp.where(keep(at[c]), lasts[c], none) for c in range(GROUP)]
        return jnp.exp(sum(kept, none))

    def always(c):
        return c >= 0

    all_f = [between(lambda c, b=b: c > b) for b in at]
    all_b = [between(lambda c, b=b: c < b) for b in at]
    mine_f = [
        jnp.where(b < place, between(lambda c, b=b: (c > b) & (c < place)), none) for b in at
    ]
    mine_b = [
        jnp.where(b > place, between(lambda c, b=b: (c < b) & (c > place)), none) for b in at
    ]
    every_f = all_f + [between(always)] + mine_f + [between(lambda c: c < place)]
    every_b = all_b + [between(always)] + mine_b + [between(lambda c: c > place)]
    pad = [none] * (16 - len(every_f))
    lines[0:16] = bdot(halves(jnp.concatenate(every_f + pad, axis=0)), widen_f[...])
    lines[16:32] = bdot(halves(jnp.concatenate(every_b + pad, axis=0)), widen_b[...])

    def f_copy(k):
        return pltpu.make_async_remote_copy(
            src_ref=snd_f.at[k], dst_ref=rcv_f.at[k], send_sem=fs_sem.at[k], recv_sem=fr_sem.at[k],
            device_id=(s + GROUP, h), device_id_type=MESH,
        )

    def b_copy(k):
        return pltpu.make_async_remote_copy(
            src_ref=snd_b.at[k], dst_ref=rcv_b.at[k], send_sem=bs_sem.at[k], recv_sem=br_sem.at[k],
            device_id=(s - GROUP, h), device_id_type=MESH,
        )

    def gathered(k, first, st, rcv):
        cols = columns(k, chunk)
        line = lines[:, cols]
        total = line[first + GROUP : first + GROUP + 1] * rcv[k].astype(F32)
        for b in range(GROUP):
            total = total + line[first + b : first + b + 1] * st[b, :, cols]
        return total.astype(BF16)

    def pass_on(k, base, st, rcv, snd, copy, got, sent):
        inside = (k >= 0) & (k < chunks)

        @pl.when(inside & got)
        def _():
            copy(k).wait_recv()

        @pl.when(inside & sent)
        def _():
            snd[k] = gathered(k, base, st, rcv)
            copy(k).start()

    lag_f = lap
    lag_b = laps - 1 - lap
    lag = jnp.maximum(lag_f, lag_b)

    def slot(n, carry):
        @pl.when(n < chunks)
        def _():
            project(n)

        pass_on(n - lag_f, 0, st_f, rcv_f, snd_f, f_copy, lap > 0, lap < laps - 1)
        pass_on(
            n - lag_b, 16, st_b, rcv_b, snd_b, b_copy, lap < laps - 1, lap > 0
        )
        k = n - lag

        @pl.when((k >= 0) & (k < chunks))
        def _():
            cols = columns(k, chunk)
            ahead = gathered(k, GROUP + 1, st_f, rcv_f)
            behind = gathered(k, 16 + GROUP + 1, st_b, rcv_b)
            scale_f = bdot(own_scale[...], widen_f[:, cols])
            scale_b = bdot(own_scale[...], widen_b[:, cols])
            result = acc[:, cols] + scale_f * bdot(own_out[0], ahead)
            result = result + scale_b * bdot(own_out[1], behind)
            out_ref[:, cols] = result.astype(out_ref.dtype)

        return carry

    lax.fori_loop(0, chunks + laps - 1, slot, 0)

    for d in range(1, GROUP):
        peer(jnp.int32(d)).wait_send()
    for d in range(GROUP):
        for e in range(1, nh):
            sib(jnp.int32(d), e, x_ref).wait_send()

    @pl.when(lap < laps - 1)
    def _():
        lax.fori_loop(0, chunks, lambda k, c: (f_copy(k).wait_send(), c)[1], 0)

    @pl.when(lap > 0)
    def _():
        lax.fori_loop(0, chunks, lambda k, c: (b_copy(k).wait_send(), c)[1], 0)


def shards(ns, nh, hidden_in, w_inner, w_inout, w_step, step_bias, decay_rate, skip_gain):
    rows, dim = hidden_in.shape
    width = w_inner.shape[1]
    heads = w_step.shape[2]
    states = w_inout.shape[1] // 4
    span = rows * nh
    tile = 512
    chunk = 256
    tiles, chunks = width // tile, width // chunk
    dma = pltpu.SemaphoreType.DMA
    vmem = pl.BlockSpec(memory_space=pltpu.VMEM)
    hbm = pl.BlockSpec(memory_space=pl.ANY)
    return pl.pallas_call(
        functools.partial(kernel, ns, nh, rows, dim, width, heads, states, tile, chunk),
        out_shape=jax.ShapeDtypeStruct((span, width), BF16),
        in_specs=[hbm, hbm, hbm, vmem, vmem, vmem, vmem],
        out_specs=vmem,
        scratch_shapes=[
            pltpu.VMEM((GROUP * span, dim), BF16),
            pltpu.VMEM((dim, width), BF16),
            pltpu.VMEM((dim, 4 * states), BF16),
            pltpu.VMEM((span, width), BF16),
            pltpu.VMEM((GROUP, states, width), F32),
            pltpu.VMEM((GROUP, states, width), F32),
            pltpu.VMEM((2, span, states), BF16),
            pltpu.VMEM((span, 4 * heads), BF16),
            pltpu.VMEM((span, width), F32),
            pltpu.VMEM((4 * heads, width), BF16),
            pltpu.VMEM((4 * heads, width), BF16),
            pltpu.VMEM((32, width), F32),
            pltpu.VMEM((2 * heads, span), F32),
            pltpu.VMEM((2 * heads, span), F32),
            pltpu.VMEM((2 * heads, span), F32),
            pltpu.VMEM(((GROUP - 1) * span, 4 * heads), BF16),
            pltpu.VMEM((2, GROUP - 1, states, span), BF16),
            pltpu.VMEM((chunks, states, chunk), BF16),
            pltpu.VMEM((chunks, states, chunk), BF16),
            pltpu.VMEM((chunks, states, chunk), BF16),
            pltpu.VMEM((chunks, states, chunk), BF16),
            dma((tiles,)),
            dma,
            dma,
            dma((GROUP - 1,)),
            dma((GROUP - 1,)),
            dma((GROUP * (nh - 1),)),
            dma((GROUP * (nh - 1),)),
            dma((chunks,)),
            dma((chunks,)),
            dma((chunks,)),
            dma((chunks,)),
        ],
        compiler_params=pltpu.CompilerParams(
            collective_id=0, has_side_effects=True, vmem_limit_bytes=56 * 1024 * 1024
        ),
    )(
        hidden_in, w_inner, w_inout,
        jnp.swapaxes(w_step, 1, 2).reshape(2 * heads, dim), step_bias,
        decay_rate.reshape(1, heads), skip_gain.reshape(1, heads),
    )


def solution(mesh):
    placed = (
        P(("seq", "head"), None),
        P(None, "head"),
        P(),
        P(None, None, "head"),
        P(None, "head"),
        P("head"),
        P("head"),
    )
    return jax.shard_map(
        functools.partial(shards, mesh.shape["seq"], mesh.shape["head"]),
        mesh=mesh, in_specs=placed, out_specs=P("seq", "head"), check_vma=False,
    )
```

```python
import functools

import jax
import jax.numpy as jnp
from jax import lax
from jax.experimental import pallas as pl
from jax.experimental.pallas import tpu as pltpu
from jax.sharding import PartitionSpec as P

HEADDIM = 64
GROUP = 4
STRIDE = 2
MESH = pl.DeviceIdType.MESH
F32 = jnp.float32
BF16 = jnp.bfloat16
EXACT = lax.Precision.HIGHEST


def bdot(a, b):
    return jnp.dot(a, b, preferred_element_type=F32)


def turned(a, b):
    return lax.dot_general(
        a, b, (((0,), (0,)), ((), ())), precision=EXACT, preferred_element_type=F32
    )


def softplus(x):
    return jnp.maximum(x, 0.0) + jnp.log1p(jnp.exp(-jnp.abs(x)))


def halves(x):
    top = x.astype(BF16).astype(F32)
    return jnp.concatenate([top, x - top], axis=1).astype(BF16)


def kernel(
    ns, nh, rows, dim, width, heads, states, tile, chunk,
    x_ref, w_hbm, wio_hbm, ws_ref, bias_ref, rate_ref, skip_ref, out_ref,
    hid, w_ref, wio_ref, inn, st_f, st_b, own_out, own_scale, acc,
    widen_f, widen_b, lines, cum_line, exc_line, step_line, tails, in_turn,
    snd_f, snd_b, rcv_f, rcv_b,
    w_sem, wio_sem, x_sem, peer_send, peer_recv, sib_send, sib_recv,
    fs_sem, fr_sem, bs_sem, br_sem,
):
    s = lax.axis_index("seq")
    h = lax.axis_index("head")
    span = rows * nh
    place = lax.rem(s, GROUP)
    lap = lax.div(s, GROUP)
    laps = ns // GROUP
    first_seq = s - place
    tiles = width // tile
    chunks = width // chunk

    def partner(d):
        px = lax.rem(lax.rem(place, 2) + lax.rem(d, 2), 2)
        py = lax.rem(lax.div(place, 2) + lax.div(d, 2), 2)
        return py * 2 + px

    def sibling(e):
        return lax.rem(h + e, nh)

    def piece(d, hh):
        return pl.ds(pl.multiple_of((d * nh + hh) * rows, rows), rows)

    def columns(t, size):
        return pl.ds(pl.multiple_of(t * size, size), size)

    def w_copy(t):
        return pltpu.make_async_copy(
            w_hbm.at[:, columns(t, tile)], w_ref.at[:, columns(t, tile)], w_sem.at[t]
        )

    own_copy = pltpu.make_async_copy(x_ref, hid.at[piece(0, h)], x_sem)
    own_copy.start()
    wio_copy = pltpu.make_async_copy(wio_hbm, wio_ref, wio_sem)
    wio_copy.start()
    for t in range(tiles):
        w_copy(jnp.int32(t)).start()

    barrier = pltpu.get_barrier_semaphore()
    for d in range(1, GROUP):
        to = first_seq + partner(jnp.int32(d))
        pl.semaphore_signal(barrier, 1, device_id=(to, h), device_id_type=MESH)
    for e in range(1, nh):
        pl.semaphore_signal(barrier, 1, device_id=(s, sibling(e)), device_id_type=MESH)

    @pl.when(lap > 0)
    def _():
        pl.semaphore_signal(barrier, 1, device_id=(s - GROUP, h), device_id_type=MESH)

    @pl.when(lap < laps - 1)
    def _():
        pl.semaphore_signal(barrier, 1, device_id=(s + GROUP, h), device_id_type=MESH)

    near = jnp.where(lap > 0, 1, 0) + jnp.where(lap < laps - 1, 1, 0)
    pl.semaphore_wait(barrier, GROUP - 1 + nh - 1 + near)

    def peer(d):
        return pltpu.make_async_remote_copy(
            src_ref=x_ref,
            dst_ref=hid.at[piece(d, h)],
            send_sem=peer_send.at[d - 1],
            recv_sem=peer_recv.at[d - 1],
            device_id=(first_seq + partner(d), h),
            device_id_type=MESH,
        )

    def sib(d, e, src):
        return pltpu.make_async_remote_copy(
            src_ref=src,
            dst_ref=hid.at[piece(d, h)],
            send_sem=sib_send.at[d * (nh - 1) + e - 1],
            recv_sem=sib_recv.at[d * (nh - 1) + e - 1],
            device_id=(s, sibling(e)),
            device_id_type=MESH,
        )

    zero = jnp.int32(0)
    for e in range(1, nh):
        sib(zero, e, x_ref).start()
    for d in range(1, GROUP):
        peer(jnp.int32(d)).start()

    @pl.when(lap == 0)
    def _():
        rcv_f[...] = jnp.zeros_like(rcv_f)

    @pl.when(lap == laps - 1)
    def _():
        rcv_b[...] = jnp.zeros_like(rcv_b)

    below = lax.broadcasted_iota(jnp.int32, (span, span), 0)
    right = lax.broadcasted_iota(jnp.int32, (span, span), 1)
    left_half = lax.broadcasted_iota(jnp.int32, (1, 128), 1) < HEADDIM
    lower = below > right
    level = below == right
    tri = jnp.where(below >= right, 1.0, 0.0).astype(F32)
    over = (((1,), (1,)), ((), ()))
    rate = jnp.concatenate([rate_ref[...], rate_ref[...]], axis=1)
    bias = jnp.concatenate([bias_ref[0:1, :], bias_ref[1:2, :]], axis=1)
    two = 2 * heads
    is_fwd = lax.broadcasted_iota(jnp.int32, (span, two), 1) < heads

    part = lax.rem(lax.broadcasted_iota(jnp.int32, (2 * two, width), 0), two) * HEADDIM
    column = lax.broadcasted_iota(jnp.int32, (2 * two, width), 1)
    widen_f[...] = jnp.where((column >= part) & (column < part + HEADDIM), 1.0, 0.0).astype(BF16)
    part = part - width
    widen_b[...] = jnp.where((column >= part) & (column < part + HEADDIM), 1.0, 0.0).astype(BF16)

    def forward(d):
        peer(d).wait_recv()
        for e in range(1, nh):
            sib(d, e, hid.at[piece(d, h)]).start()

    def prepare(xb):
        maps = bdot(xb, wio_ref[...]).astype(BF16)
        steps = softplus(
            lax.dot_general(xb, ws_ref[...], over, preferred_element_type=F32) + bias
        )
        return maps, steps, -rate * steps

    def sums(steps, logs):
        cum = jnp.dot(tri, logs, precision=EXACT, preferred_element_type=F32)
        exc = cum - logs
        last = cum[span - 1 : span, :]
        tail = jnp.exp(jnp.where(is_fwd, last - cum, exc)) * steps
        return cum, exc, last, halves(tail)

    def turn(m):
        return m.astype(F32).T.astype(BF16)

    own_copy.wait()
    for e in range(1, nh):
        sib(zero, e, x_ref).wait_recv()
    wio_copy.wait()
    maps, steps, logs = prepare(hid[0:span, :])
    cum, exc, last_own, tail_own = sums(steps, logs)
    in_f = turn(maps[:, :states])
    in_b = turn(maps[:, 2 * states : 3 * states])

    def project_own(t, carry):
        cols = columns(t, tile)
        w_copy(t).wait()
        values = bdot(hid[0:span, :], w_ref[:, cols]).astype(BF16)
        inn[:, cols] = values
        wide = values.astype(F32)
        st_f[0, :, cols] = bdot(in_f, (bdot(tail_own, widen_f[:, cols]) * wide).astype(BF16))
        st_b[0, :, cols] = bdot(in_b, (bdot(tail_own, widen_b[:, cols]) * wide).astype(BF16))
        return carry

    lax.fori_loop(0, tiles, project_own, 0)
    forward(jnp.int32(1))

    out_f = maps[:, states : 2 * states]
    out_b = maps[:, 3 * states :]
    own_out[0] = out_f
    own_out[1] = out_b
    own_scale[...] = halves(jnp.exp(jnp.where(is_fwd, cum, last_own - exc)))
    score = jnp.where(
        lower,
        lax.dot_general(out_f, maps[:, :states], over, preferred_element_type=F32),
        lax.dot_general(
            out_b, maps[:, 2 * states : 3 * states], over, preferred_element_type=F32
        ),
    )
    score = jnp.where(level, 0.0, score)
    unit = jnp.where(level, 1.0, 0.0).astype(F32)
    cum_line[...] = turned(cum, unit)
    exc_line[...] = turned(exc, unit)
    step_line[...] = turned(steps, unit)
    cum_two = halves(cum)
    exc_two = halves(exc)
    skip_two = halves(
        jnp.broadcast_to(jnp.concatenate([skip_ref[...], skip_ref[...]], axis=1), (8, two))
    )
    owner = lax.rem(lax.broadcasted_iota(jnp.int32, (2 * two, 128), 0), two)

    def mix(i, carry):
        cols = columns(i, 128)
        both = inn[:, cols]
        parts = []
        for k in (2 * i, 2 * i + 1):
            pick_f = jnp.where(owner == k, 1.0, 0.0).astype(BF16)
            pick_b = jnp.where(owner == k + heads, 1.0, 0.0).astype(BF16)
            fwd = pl.ds(k, 1)
            bwd = pl.ds(k + heads, 1)
            gap = jnp.where(
                lower,
                bdot(cum_two, pick_f) - cum_line[fwd, :],
                exc_line[bwd, :] - bdot(exc_two, pick_b),
            )
            scale = jnp.where(lower, step_line[fwd, :], step_line[bwd, :])
            parts.append(bdot((jnp.exp(gap) * (score * scale)).astype(BF16), both))
        gain = bdot(skip_two, widen_f[:, cols])[0:1, :]
        acc[:, cols] = jnp.where(left_half, parts[0], parts[1]) + gain * both.astype(F32)
        return carry

    lax.fori_loop(0, heads // 4, mix, 0, unroll=min(4, heads // 4))
    for d in range(2, GROUP):
        forward(jnp.int32(d))
    lax.fori_loop(heads // 4, heads // 2, mix, 0, unroll=min(4, heads // 4))

    for d in range(1, GROUP):
        for e in range(1, nh):
            sib(jnp.int32(d), e, x_ref).wait_recv()
    maps, steps, logs = prepare(hid[span:, :])
    lasts = [last_own]
    for d in range(1, GROUP):
        mine = slice((d - 1) * span, d * span)
        _, _, last, tail = sums(steps[mine], logs[mine])
        lasts.append(last)
        tails[mine, :] = tail
        in_turn[0, d - 1] = turn(maps[mine, :states])
        in_turn[1, d - 1] = turn(maps[mine, 2 * states : 3 * states])

    def project(k):
        cols = columns(k, chunk)
        wide = bdot(hid[span:, :], w_ref[:, cols]).astype(BF16).astype(F32)
        for way, grow, st in ((0, widen_f, st_f), (1, widen_b, st_b)):
            scaled = (bdot(tails[...], grow[:, cols]) * wide).astype(BF16)
            for d in range(1, GROUP):
                st[d, :, cols] = bdot(in_turn[way, d - 1], scaled[(d - 1) * span : d * span])

    at = [partner(jnp.int32(d)) for d in range(GROUP)]
    none = jnp.zeros_like(last_own)

    def between(keep):
        kept = [jnp.where(keep(at[c]), lasts[c], none) for c in range(GROUP)]
        return jnp.exp(sum(kept, none))

    def always(c):
        return c >= 0

    all_f = [between(lambda c, b=b: c > b) for b in at]
    all_b = [between(lambda c, b=b: c < b) for b in at]
    mine_f = [
        jnp.where(b < place, between(lambda c, b=b: (c > b) & (c < place)), none) for b in at
    ]
    mine_b = [
        jnp.where(b > place, between(lambda c, b=b: (c < b) & (c > place)), none) for b in at
    ]
    every_f = all_f + [between(always)] + mine_f + [between(lambda c: c < place)]
    every_b = all_b + [between(always)] + mine_b + [between(lambda c: c > place)]
    pad = [none] * (16 - len(every_f))
    lines[0:16] = bdot(halves(jnp.concatenate(every_f + pad, axis=0)), widen_f[...])
    lines[16:32] = bdot(halves(jnp.concatenate(every_b + pad, axis=0)), widen_b[...])

    def f_copy(k):
        return pltpu.make_async_remote_copy(
            src_ref=snd_f.at[k], dst_ref=rcv_f.at[k], send_sem=fs_sem.at[k], recv_sem=fr_sem.at[k],
            device_id=(s + GROUP, h), device_id_type=MESH,
        )

    def b_copy(k):
        return pltpu.make_async_remote_copy(
            src_ref=snd_b.at[k], dst_ref=rcv_b.at[k], send_sem=bs_sem.at[k], recv_sem=br_sem.at[k],
            device_id=(s - GROUP, h), device_id_type=MESH,
        )

    def gathered(k, first, st, rcv):
        cols = columns(k, chunk)
        line = lines[:, cols]
        total = line[first + GROUP : first + GROUP + 1] * rcv[k].astype(F32)
        for b in range(GROUP):
            total = total + line[first + b : first + b + 1] * st[b, :, cols]
        return total.astype(BF16)

    def pass_on(k, base, st, rcv, snd, copy, got, sent):
        inside = (k >= 0) & (k < chunks)

        @pl.when(inside & got)
        def _():
            copy(k).wait_recv()

        @pl.when(inside & sent)
        def _():
            snd[k] = gathered(k, base, st, rcv)
            copy(k).start()

    lag_f = STRIDE * lap
    lag_b = STRIDE * (laps - 1 - lap)
    lag = jnp.maximum(lag_f, lag_b)

    def slot(n, carry):
        pass_on(n - lag_f, 0, st_f, rcv_f, snd_f, f_copy, lap > 0, lap < laps - 1)
        pass_on(
            n - lag_b, 16, st_b, rcv_b, snd_b, b_copy, lap < laps - 1, lap > 0
        )
        k = n - lag

        @pl.when(n < chunks - 1)
        def _():
            project(n + 1)

        @pl.when((k >= 0) & (k < chunks))
        def _():
            cols = columns(k, chunk)
            ahead = gathered(k, GROUP + 1, st_f, rcv_f)
            behind = gathered(k, 16 + GROUP + 1, st_b, rcv_b)
            scale_f = bdot(own_scale[...], widen_f[:, cols])
            scale_b = bdot(own_scale[...], widen_b[:, cols])
            result = acc[:, cols] + scale_f * bdot(own_out[0], ahead)
            result = result + scale_b * bdot(own_out[1], behind)
            out_ref[:, cols] = result.astype(out_ref.dtype)

        return carry

    project(zero)
    lax.fori_loop(0, chunks + STRIDE * (laps - 1), slot, 0)

    for d in range(1, GROUP):
        peer(jnp.int32(d)).wait_send()
    for d in range(GROUP):
        for e in range(1, nh):
            sib(jnp.int32(d), e, x_ref).wait_send()

    @pl.when(lap < laps - 1)
    def _():
        lax.fori_loop(0, chunks, lambda k, c: (f_copy(k).wait_send(), c)[1], 0)

    @pl.when(lap > 0)
    def _():
        lax.fori_loop(0, chunks, lambda k, c: (b_copy(k).wait_send(), c)[1], 0)


def shards(ns, nh, hidden_in, w_inner, w_inout, w_step, step_bias, decay_rate, skip_gain):
    rows, dim = hidden_in.shape
    width = w_inner.shape[1]
    heads = w_step.shape[2]
    states = w_inout.shape[1] // 4
    span = rows * nh
    tile = 512
    chunk = 256
    tiles, chunks = width // tile, width // chunk
    dma = pltpu.SemaphoreType.DMA
    vmem = pl.BlockSpec(memory_space=pltpu.VMEM)
    hbm = pl.BlockSpec(memory_space=pl.ANY)
    return pl.pallas_call(
        functools.partial(kernel, ns, nh, rows, dim, width, heads, states, tile, chunk),
        out_shape=jax.ShapeDtypeStruct((span, width), BF16),
        in_specs=[hbm, hbm, hbm, vmem, vmem, vmem, vmem],
        out_specs=vmem,
        scratch_shapes=[
            pltpu.VMEM((GROUP * span, dim), BF16),
            pltpu.VMEM((dim, width), BF16),
            pltpu.VMEM((dim, 4 * states), BF16),
            pltpu.VMEM((span, width), BF16),
            pltpu.VMEM((GROUP, states, width), F32),
            pltpu.VMEM((GROUP, states, width), F32),
            pltpu.VMEM((2, span, states), BF16),
            pltpu.VMEM((span, 4 * heads), BF16),
            pltpu.VMEM((span, width), F32),
            pltpu.VMEM((4 * heads, width), BF16),
            pltpu.VMEM((4 * heads, width), BF16),
            pltpu.VMEM((32, width), F32),
            pltpu.VMEM((2 * heads, span), F32),
            pltpu.VMEM((2 * heads, span), F32),
            pltpu.VMEM((2 * heads, span), F32),
            pltpu.VMEM(((GROUP - 1) * span, 4 * heads), BF16),
            pltpu.VMEM((2, GROUP - 1, states, span), BF16),
            pltpu.VMEM((chunks, states, chunk), BF16),
            pltpu.VMEM((chunks, states, chunk), BF16),
            pltpu.VMEM((chunks, states, chunk), BF16),
            pltpu.VMEM((chunks, states, chunk), BF16),
            dma((tiles,)),
            dma,
            dma,
            dma((GROUP - 1,)),
            dma((GROUP - 1,)),
            dma((GROUP * (nh - 1),)),
            dma((GROUP * (nh - 1),)),
            dma((chunks,)),
            dma((chunks,)),
            dma((chunks,)),
            dma((chunks,)),
        ],
        compiler_params=pltpu.CompilerParams(
            collective_id=0, has_side_effects=True, vmem_limit_bytes=56 * 1024 * 1024
        ),
    )(
        hidden_in, w_inner, w_inout,
        jnp.swapaxes(w_step, 1, 2).reshape(2 * heads, dim), step_bias,
        decay_rate.reshape(1, heads), skip_gain.reshape(1, heads),
    )


def solution(mesh):
    placed = (
        P(("seq", "head"), None),
        P(None, "head"),
        P(),
        P(None, None, "head"),
        P(None, "head"),
        P("head"),
        P("head"),
    )
    return jax.shard_map(
        functools.partial(shards, mesh.shape["seq"], mesh.shape["head"]),
        mesh=mesh, in_specs=placed, out_specs=P("seq", "head"), check_vma=False,
    )
```

```python
import functools

import jax
import jax.numpy as jnp
from jax import lax
from jax.experimental import pallas as pl
from jax.experimental.pallas import tpu as pltpu
from jax.sharding import PartitionSpec as P

HEADDIM = 64
GROUP = 4
STRIDE = 2
MESH = pl.DeviceIdType.MESH
F32 = jnp.float32
BF16 = jnp.bfloat16
EXACT = lax.Precision.HIGHEST


def bdot(a, b):
    return jnp.dot(a, b, preferred_element_type=F32)


def turned(a, b):
    return lax.dot_general(
        a, b, (((0,), (0,)), ((), ())), precision=EXACT, preferred_element_type=F32
    )


def softplus(x):
    return jnp.maximum(x, 0.0) + jnp.log1p(jnp.exp(-jnp.abs(x)))


def halves(x):
    top = x.astype(BF16).astype(F32)
    return jnp.concatenate([top, x - top], axis=1).astype(BF16)


def kernel(
    ns, nh, rows, dim, width, heads, states, tile, chunk,
    x_ref, w_hbm, wio_hbm, ws_ref, bias_ref, rate_ref, skip_ref, out_ref,
    hid, w_ref, wio_ref, inn, st_f, st_b, own_out, own_scale,
    widen_f, widen_b, lines, cum_line, exc_line, step_line, tails, in_turn,
    snd_f, snd_b, rcv_f, rcv_b,
    w_sem, wio_sem, x_sem, peer_send, peer_recv, sib_send, sib_recv,
    fs_sem, fr_sem, bs_sem, br_sem,
):
    s = lax.axis_index("seq")
    h = lax.axis_index("head")
    span = rows * nh
    place = lax.rem(s, GROUP)
    lap = lax.div(s, GROUP)
    laps = ns // GROUP
    first_seq = s - place
    tiles = width // tile
    chunks = width // chunk

    def partner(d):
        px = lax.rem(lax.rem(place, 2) + lax.rem(d, 2), 2)
        py = lax.rem(lax.div(place, 2) + lax.div(d, 2), 2)
        return py * 2 + px

    def sibling(e):
        return lax.rem(h + e, nh)

    def piece(d, hh):
        return pl.ds(pl.multiple_of((d * nh + hh) * rows, rows), rows)

    def columns(t, size):
        return pl.ds(pl.multiple_of(t * size, size), size)

    def w_copy(t):
        return pltpu.make_async_copy(
            w_hbm.at[:, columns(t, tile)], w_ref.at[:, columns(t, tile)], w_sem.at[t]
        )

    own_copy = pltpu.make_async_copy(x_ref, hid.at[piece(0, h)], x_sem)
    own_copy.start()
    wio_copy = pltpu.make_async_copy(wio_hbm, wio_ref, wio_sem)
    wio_copy.start()
    for t in range(tiles):
        w_copy(jnp.int32(t)).start()

    barrier = pltpu.get_barrier_semaphore()
    for d in range(1, GROUP):
        to = first_seq + partner(jnp.int32(d))
        pl.semaphore_signal(barrier, 1, device_id=(to, h), device_id_type=MESH)
    for e in range(1, nh):
        pl.semaphore_signal(barrier, 1, device_id=(s, sibling(e)), device_id_type=MESH)

    @pl.when(lap > 0)
    def _():
        pl.semaphore_signal(barrier, 1, device_id=(s - GROUP, h), device_id_type=MESH)

    @pl.when(lap < laps - 1)
    def _():
        pl.semaphore_signal(barrier, 1, device_id=(s + GROUP, h), device_id_type=MESH)

    near = jnp.where(lap > 0, 1, 0) + jnp.where(lap < laps - 1, 1, 0)
    pl.semaphore_wait(barrier, GROUP - 1 + nh - 1 + near)

    def peer(d):
        return pltpu.make_async_remote_copy(
            src_ref=x_ref,
            dst_ref=hid.at[piece(d, h)],
            send_sem=peer_send.at[d - 1],
            recv_sem=peer_recv.at[d - 1],
            device_id=(first_seq + partner(d), h),
            device_id_type=MESH,
        )

    def sib(d, e, src):
        return pltpu.make_async_remote_copy(
            src_ref=src,
            dst_ref=hid.at[piece(d, h)],
            send_sem=sib_send.at[d * (nh - 1) + e - 1],
            recv_sem=sib_recv.at[d * (nh - 1) + e - 1],
            device_id=(s, sibling(e)),
            device_id_type=MESH,
        )

    zero = jnp.int32(0)
    for e in range(1, nh):
        sib(zero, e, x_ref).start()
    for d in range(1, GROUP):
        peer(jnp.int32(d)).start()

    @pl.when(lap == 0)
    def _():
        rcv_f[...] = jnp.zeros_like(rcv_f)

    @pl.when(lap == laps - 1)
    def _():
        rcv_b[...] = jnp.zeros_like(rcv_b)

    below = lax.broadcasted_iota(jnp.int32, (span, span), 0)
    right = lax.broadcasted_iota(jnp.int32, (span, span), 1)
    left_half = lax.broadcasted_iota(jnp.int32, (1, 128), 1) < HEADDIM
    lower = below > right
    level = below == right
    tri = jnp.where(below >= right, 1.0, 0.0).astype(F32)
    over = (((1,), (1,)), ((), ()))
    rate = jnp.concatenate([rate_ref[...], rate_ref[...]], axis=1)
    bias = jnp.concatenate([bias_ref[0:1, :], bias_ref[1:2, :]], axis=1)
    two = 2 * heads
    is_fwd = lax.broadcasted_iota(jnp.int32, (span, two), 1) < heads

    part = lax.rem(lax.broadcasted_iota(jnp.int32, (2 * two, width), 0), two) * HEADDIM
    column = lax.broadcasted_iota(jnp.int32, (2 * two, width), 1)
    widen_f[...] = jnp.where((column >= part) & (column < part + HEADDIM), 1.0, 0.0).astype(BF16)
    part = part - width
    widen_b[...] = jnp.where((column >= part) & (column < part + HEADDIM), 1.0, 0.0).astype(BF16)

    def forward(d):
        peer(d).wait_recv()
        for e in range(1, nh):
            sib(d, e, hid.at[piece(d, h)]).start()

    def prepare(xb):
        maps = bdot(xb, wio_ref[...]).astype(BF16)
        steps = softplus(
            lax.dot_general(xb, ws_ref[...], over, preferred_element_type=F32) + bias
        )
        return maps, steps, -rate * steps

    def sums(steps, logs):
        cum = jnp.dot(tri, logs, precision=EXACT, preferred_element_type=F32)
        exc = cum - logs
        last = cum[span - 1 : span, :]
        tail = jnp.exp(jnp.where(is_fwd, last - cum, exc)) * steps
        return cum, exc, last, halves(tail)

    def turn(m):
        return m.astype(F32).T.astype(BF16)

    own_copy.wait()
    for e in range(1, nh):
        sib(zero, e, x_ref).wait_recv()
    wio_copy.wait()
    maps, steps, logs = prepare(hid[0:span, :])
    cum, exc, last_own, tail_own = sums(steps, logs)
    in_f = turn(maps[:, :states])
    in_b = turn(maps[:, 2 * states : 3 * states])

    def project_own(t, carry):
        cols = columns(t, tile)
        w_copy(t).wait()
        values = bdot(hid[0:span, :], w_ref[:, cols]).astype(BF16)
        inn[:, cols] = values
        wide = values.astype(F32)
        st_f[0, :, cols] = bdot(in_f, (bdot(tail_own, widen_f[:, cols]) * wide).astype(BF16))
        st_b[0, :, cols] = bdot(in_b, (bdot(tail_own, widen_b[:, cols]) * wide).astype(BF16))
        return carry

    lax.fori_loop(0, tiles, project_own, 0)
    forward(jnp.int32(1))

    out_f = maps[:, states : 2 * states]
    out_b = maps[:, 3 * states :]
    own_out[0] = out_f
    own_out[1] = out_b
    own_scale[...] = halves(jnp.exp(jnp.where(is_fwd, cum, last_own - exc)))
    score = jnp.where(
        lower,
        lax.dot_general(out_f, maps[:, :states], over, preferred_element_type=F32),
        lax.dot_general(
            out_b, maps[:, 2 * states : 3 * states], over, preferred_element_type=F32
        ),
    )
    score = jnp.where(level, 0.0, score)
    unit = jnp.where(level, 1.0, 0.0).astype(F32)
    cum_line[...] = turned(cum, unit)
    exc_line[...] = turned(exc, unit)
    step_line[...] = turned(steps, unit)
    cum_two = halves(cum)
    exc_two = halves(exc)
    skip_two = halves(
        jnp.broadcast_to(jnp.concatenate([skip_ref[...], skip_ref[...]], axis=1), (8, two))
    )
    owner = lax.rem(lax.broadcasted_iota(jnp.int32, (2 * two, 128), 0), two)

    def mix(i):
        cols = columns(i, 128)
        both = inn[:, cols]
        parts = []
        for k in (2 * i, 2 * i + 1):
            pick_f = jnp.where(owner == k, 1.0, 0.0).astype(BF16)
            pick_b = jnp.where(owner == k + heads, 1.0, 0.0).astype(BF16)
            fwd = pl.ds(k, 1)
            bwd = pl.ds(k + heads, 1)
            gap = jnp.where(
                lower,
                bdot(cum_two, pick_f) - cum_line[fwd, :],
                exc_line[bwd, :] - bdot(exc_two, pick_b),
            )
            scale = jnp.where(lower, step_line[fwd, :], step_line[bwd, :])
            parts.append(bdot((jnp.exp(gap) * (score * scale)).astype(BF16), both))
        gain = bdot(skip_two, widen_f[:, cols])[0:1, :]
        return jnp.where(left_half, parts[0], parts[1]) + gain * both.astype(F32)

    lasts = [last_own]

    def arrived(d):
        for e in range(1, nh):
            sib(jnp.int32(d), e, x_ref).wait_recv()
        maps, steps, logs = prepare(hid[d * span : (d + 1) * span, :])
        _, _, last, tail = sums(steps, logs)
        lasts.append(last)
        tails[(d - 1) * span : d * span, :] = tail
        in_turn[0, d - 1] = turn(maps[:, :states])
        in_turn[1, d - 1] = turn(maps[:, 2 * states : 3 * states])

    for d in range(1, GROUP):
        if d < GROUP - 1:
            forward(jnp.int32(d + 1))
        arrived(d)

    def project(k):
        cols = columns(k, chunk)
        wide = bdot(hid[span:, :], w_ref[:, cols]).astype(BF16).astype(F32)
        for way, grow, st in ((0, widen_f, st_f), (1, widen_b, st_b)):
            scaled = (bdot(tails[...], grow[:, cols]) * wide).astype(BF16)
            for d in range(1, GROUP):
                st[d, :, cols] = bdot(in_turn[way, d - 1], scaled[(d - 1) * span : d * span])

    at = [partner(jnp.int32(d)) for d in range(GROUP)]
    none = jnp.zeros_like(last_own)

    def between(keep):
        kept = [jnp.where(keep(at[c]), lasts[c], none) for c in range(GROUP)]
        return jnp.exp(sum(kept, none))

    def always(c):
        return c >= 0

    all_f = [between(lambda c, b=b: c > b) for b in at]
    all_b = [between(lambda c, b=b: c < b) for b in at]
    mine_f = [
        jnp.where(b < place, between(lambda c, b=b: (c > b) & (c < place)), none) for b in at
    ]
    mine_b = [
        jnp.where(b > place, between(lambda c, b=b: (c < b) & (c > place)), none) for b in at
    ]
    every_f = all_f + [between(always)] + mine_f + [between(lambda c: c < place)]
    every_b = all_b + [between(always)] + mine_b + [between(lambda c: c > place)]
    pad = [none] * (16 - len(every_f))
    lines[0:16] = bdot(halves(jnp.concatenate(every_f + pad, axis=0)), widen_f[...])
    lines[16:32] = bdot(halves(jnp.concatenate(every_b + pad, axis=0)), widen_b[...])

    def f_copy(k):
        return pltpu.make_async_remote_copy(
            src_ref=snd_f.at[k], dst_ref=rcv_f.at[k], send_sem=fs_sem.at[k], recv_sem=fr_sem.at[k],
            device_id=(s + GROUP, h), device_id_type=MESH,
        )

    def b_copy(k):
        return pltpu.make_async_remote_copy(
            src_ref=snd_b.at[k], dst_ref=rcv_b.at[k], send_sem=bs_sem.at[k], recv_sem=br_sem.at[k],
            device_id=(s - GROUP, h), device_id_type=MESH,
        )

    def gathered(k, first, st, rcv):
        cols = columns(k, chunk)
        line = lines[:, cols]
        total = line[first + GROUP : first + GROUP + 1] * rcv[k].astype(F32)
        for b in range(GROUP):
            total = total + line[first + b : first + b + 1] * st[b, :, cols]
        return total.astype(BF16)

    def pass_on(k, base, st, rcv, snd, copy, got, sent):
        inside = (k >= 0) & (k < chunks)

        @pl.when(inside & got)
        def _():
            copy(k).wait_recv()

        @pl.when(inside & sent)
        def _():
            snd[k] = gathered(k, base, st, rcv)
            copy(k).start()

    lag_f = STRIDE * lap
    lag_b = STRIDE * (laps - 1 - lap)
    lag = jnp.maximum(lag_f, lag_b)

    def slot(n, carry):
        pass_on(n - lag_f, 0, st_f, rcv_f, snd_f, f_copy, lap > 0, lap < laps - 1)
        pass_on(
            n - lag_b, 16, st_b, rcv_b, snd_b, b_copy, lap < laps - 1, lap > 0
        )
        k = n - lag

        @pl.when(n < chunks - 1)
        def _():
            project(n + 1)

        @pl.when((k >= 0) & (k < chunks))
        def _():
            cols = columns(k, chunk)
            ahead = gathered(k, GROUP + 1, st_f, rcv_f)
            behind = gathered(k, 16 + GROUP + 1, st_b, rcv_b)
            scale_f = bdot(own_scale[...], widen_f[:, cols])
            scale_b = bdot(own_scale[...], widen_b[:, cols])
            pairs = chunk // 128
            local = jnp.concatenate([mix(k * pairs + i) for i in range(pairs)], axis=1)
            result = local + scale_f * bdot(own_out[0], ahead)
            result = result + scale_b * bdot(own_out[1], behind)
            out_ref[:, cols] = result.astype(out_ref.dtype)

        return carry

    project(zero)
    lax.fori_loop(0, chunks + STRIDE * (laps - 1), slot, 0)

    for d in range(1, GROUP):
        peer(jnp.int32(d)).wait_send()
    for d in range(GROUP):
        for e in range(1, nh):
            sib(jnp.int32(d), e, x_ref).wait_send()

    @pl.when(lap < laps - 1)
    def _():
        lax.fori_loop(0, chunks, lambda k, c: (f_copy(k).wait_send(), c)[1], 0)

    @pl.when(lap > 0)
    def _():
        lax.fori_loop(0, chunks, lambda k, c: (b_copy(k).wait_send(), c)[1], 0)


def shards(ns, nh, hidden_in, w_inner, w_inout, w_step, step_bias, decay_rate, skip_gain):
    rows, dim = hidden_in.shape
    width = w_inner.shape[1]
    heads = w_step.shape[2]
    states = w_inout.shape[1] // 4
    span = rows * nh
    tile = 512
    chunk = 256
    tiles, chunks = width // tile, width // chunk
    dma = pltpu.SemaphoreType.DMA
    vmem = pl.BlockSpec(memory_space=pltpu.VMEM)
    hbm = pl.BlockSpec(memory_space=pl.ANY)
    return pl.pallas_call(
        functools.partial(kernel, ns, nh, rows, dim, width, heads, states, tile, chunk),
        out_shape=jax.ShapeDtypeStruct((span, width), BF16),
        in_specs=[hbm, hbm, hbm, vmem, vmem, vmem, vmem],
        out_specs=vmem,
        scratch_shapes=[
            pltpu.VMEM((GROUP * span, dim), BF16),
            pltpu.VMEM((dim, width), BF16),
            pltpu.VMEM((dim, 4 * states), BF16),
            pltpu.VMEM((span, width), BF16),
            pltpu.VMEM((GROUP, states, width), F32),
            pltpu.VMEM((GROUP, states, width), F32),
            pltpu.VMEM((2, span, states), BF16),
            pltpu.VMEM((span, 4 * heads), BF16),
            pltpu.VMEM((4 * heads, width), BF16),
            pltpu.VMEM((4 * heads, width), BF16),
            pltpu.VMEM((32, width), F32),
            pltpu.VMEM((2 * heads, span), F32),
            pltpu.VMEM((2 * heads, span), F32),
            pltpu.VMEM((2 * heads, span), F32),
            pltpu.VMEM(((GROUP - 1) * span, 4 * heads), BF16),
            pltpu.VMEM((2, GROUP - 1, states, span), BF16),
            pltpu.VMEM((chunks, states, chunk), BF16),
            pltpu.VMEM((chunks, states, chunk), BF16),
            pltpu.VMEM((chunks, states, chunk), BF16),
            pltpu.VMEM((chunks, states, chunk), BF16),
            dma((tiles,)),
            dma,
            dma,
            dma((GROUP - 1,)),
            dma((GROUP - 1,)),
            dma((GROUP * (nh - 1),)),
            dma((GROUP * (nh - 1),)),
            dma((chunks,)),
            dma((chunks,)),
            dma((chunks,)),
            dma((chunks,)),
        ],
        compiler_params=pltpu.CompilerParams(
            collective_id=0, has_side_effects=True, vmem_limit_bytes=56 * 1024 * 1024
        ),
    )(
        hidden_in, w_inner, w_inout,
        jnp.swapaxes(w_step, 1, 2).reshape(2 * heads, dim), step_bias,
        decay_rate.reshape(1, heads), skip_gain.reshape(1, heads),
    )


def solution(mesh):
    placed = (
        P(("seq", "head"), None),
        P(None, "head"),
        P(),
        P(None, None, "head"),
        P(None, "head"),
        P("head"),
        P("head"),
    )
    return jax.shard_map(
        functools.partial(shards, mesh.shape["seq"], mesh.shape["head"]),
        mesh=mesh, in_specs=placed, out_specs=P("seq", "head"), check_vma=False,
    )
```

```python
import functools

import jax
import jax.numpy as jnp
from jax import lax
from jax.experimental import pallas as pl
from jax.experimental.pallas import tpu as pltpu
from jax.sharding import PartitionSpec as P

HEADDIM = 64
GROUP = 4
STRIDE = 2
MESH = pl.DeviceIdType.MESH
F32 = jnp.float32
BF16 = jnp.bfloat16
EXACT = lax.Precision.HIGHEST


def bdot(a, b):
    return jnp.dot(a, b, preferred_element_type=F32)


def turned(a, b):
    return lax.dot_general(
        a, b, (((0,), (0,)), ((), ())), precision=EXACT, preferred_element_type=F32
    )


def softplus(x):
    return jnp.maximum(x, 0.0) + jnp.log1p(jnp.exp(-jnp.abs(x)))


def halves(x):
    top = x.astype(BF16).astype(F32)
    return jnp.concatenate([top, x - top], axis=1).astype(BF16)


def kernel(
    ns, nh, rows, dim, width, heads, states, tile, chunk,
    x_ref, w_hbm, wio_hbm, ws_ref, bias_ref, rate_ref, skip_ref, out_ref,
    hid, w_ref, wio_ref, inn, st_f, st_b, own_out, own_scale,
    widen_f, widen_b, lines, cum_line, exc_line, step_line, tails, in_turn,
    snd_f, snd_b, rcv_f, rcv_b,
    w_sem, wio_sem, x_sem, peer_send, peer_recv, sib_send, sib_recv,
    fs_sem, fr_sem, bs_sem, br_sem,
):
    s = lax.axis_index("seq")
    h = lax.axis_index("head")
    span = rows * nh
    place = lax.rem(s, GROUP)
    lap = lax.div(s, GROUP)
    laps = ns // GROUP
    first_seq = s - place
    tiles = width // tile
    chunks = width // chunk

    def partner(d):
        px = lax.rem(lax.rem(place, 2) + lax.rem(d, 2), 2)
        py = lax.rem(lax.div(place, 2) + lax.div(d, 2), 2)
        return py * 2 + px

    def sibling(e):
        return lax.rem(h + e, nh)

    def piece(d, hh):
        return pl.ds(pl.multiple_of((d * nh + hh) * rows, rows), rows)

    def columns(t, size):
        return pl.ds(pl.multiple_of(t * size, size), size)

    def w_copy(t):
        return pltpu.make_async_copy(
            w_hbm.at[:, columns(t, tile)], w_ref.at[:, columns(t, tile)], w_sem.at[t]
        )

    own_copy = pltpu.make_async_copy(x_ref, hid.at[piece(0, h)], x_sem)
    own_copy.start()
    wio_copy = pltpu.make_async_copy(wio_hbm, wio_ref, wio_sem)
    wio_copy.start()
    for t in range(tiles):
        w_copy(jnp.int32(t)).start()

    barrier = pltpu.get_barrier_semaphore()
    for d in range(1, GROUP):
        to = first_seq + partner(jnp.int32(d))
        pl.semaphore_signal(barrier, 1, device_id=(to, h), device_id_type=MESH)
    for e in range(1, nh):
        pl.semaphore_signal(barrier, 1, device_id=(s, sibling(e)), device_id_type=MESH)

    @pl.when(lap > 0)
    def _():
        pl.semaphore_signal(barrier, 1, device_id=(s - GROUP, h), device_id_type=MESH)

    @pl.when(lap < laps - 1)
    def _():
        pl.semaphore_signal(barrier, 1, device_id=(s + GROUP, h), device_id_type=MESH)

    near = jnp.where(lap > 0, 1, 0) + jnp.where(lap < laps - 1, 1, 0)
    pl.semaphore_wait(barrier, GROUP - 1 + nh - 1 + near)

    def peer(d, src=x_ref, to=None):
        return pltpu.make_async_remote_copy(
            src_ref=src,
            dst_ref=hid.at[piece(d, h)],
            send_sem=peer_send.at[d - 1],
            recv_sem=peer_recv.at[d - 1],
            device_id=(first_seq + partner(d if to is None else to), h),
            device_id_type=MESH,
        )

    def relay():
        first = 1 + lax.rem(h, 2)
        peer(first).wait_recv()
        peer(jnp.int32(3), hid.at[piece(first, h)], 3 - first).start()
        second = 3 - first
        peer(second).wait_recv()
        for d in (first, second):
            for e in range(1, nh):
                sib(d, e, hid.at[piece(d, h)]).start()

    def sib(d, e, src):
        return pltpu.make_async_remote_copy(
            src_ref=src,
            dst_ref=hid.at[piece(d, h)],
            send_sem=sib_send.at[d * (nh - 1) + e - 1],
            recv_sem=sib_recv.at[d * (nh - 1) + e - 1],
            device_id=(s, sibling(e)),
            device_id_type=MESH,
        )

    zero = jnp.int32(0)
    for e in range(1, nh):
        sib(zero, e, x_ref).start()
    for d in (1, 2):
        peer(jnp.int32(d)).start()

    @pl.when(lap == 0)
    def _():
        rcv_f[...] = jnp.zeros_like(rcv_f)

    @pl.when(lap == laps - 1)
    def _():
        rcv_b[...] = jnp.zeros_like(rcv_b)

    below = lax.broadcasted_iota(jnp.int32, (span, span), 0)
    right = lax.broadcasted_iota(jnp.int32, (span, span), 1)
    left_half = lax.broadcasted_iota(jnp.int32, (1, 128), 1) < HEADDIM
    lower = below > right
    level = below == right
    tri = jnp.where(below >= right, 1.0, 0.0).astype(F32)
    over = (((1,), (1,)), ((), ()))
    rate = jnp.concatenate([rate_ref[...], rate_ref[...]], axis=1)
    bias = jnp.concatenate([bias_ref[0:1, :], bias_ref[1:2, :]], axis=1)
    two = 2 * heads
    is_fwd = lax.broadcasted_iota(jnp.int32, (span, two), 1) < heads

    part = lax.rem(lax.broadcasted_iota(jnp.int32, (2 * two, width), 0), two) * HEADDIM
    column = lax.broadcasted_iota(jnp.int32, (2 * two, width), 1)
    widen_f[...] = jnp.where((column >= part) & (column < part + HEADDIM), 1.0, 0.0).astype(BF16)
    part = part - width
    widen_b[...] = jnp.where((column >= part) & (column < part + HEADDIM), 1.0, 0.0).astype(BF16)

    def forward(d):
        peer(d).wait_recv()
        for e in range(1, nh):
            sib(d, e, hid.at[piece(d, h)]).start()

    def prepare(xb):
        maps = bdot(xb, wio_ref[...]).astype(BF16)
        steps = softplus(
            lax.dot_general(xb, ws_ref[...], over, preferred_element_type=F32) + bias
        )
        return maps, steps, -rate * steps

    def sums(steps, logs):
        cum = jnp.dot(tri, logs, precision=EXACT, preferred_element_type=F32)
        exc = cum - logs
        last = cum[span - 1 : span, :]
        tail = jnp.exp(jnp.where(is_fwd, last - cum, exc)) * steps
        return cum, exc, last, halves(tail)

    def turn(m):
        return m.astype(F32).T.astype(BF16)

    own_copy.wait()
    for e in range(1, nh):
        sib(zero, e, x_ref).wait_recv()
    wio_copy.wait()
    maps, steps, logs = prepare(hid[0:span, :])
    relay()
    cum, exc, last_own, tail_own = sums(steps, logs)
    in_f = turn(maps[:, :states])
    in_b = turn(maps[:, 2 * states : 3 * states])

    def project_own(t, carry):
        cols = columns(t, tile)
        w_copy(t).wait()
        values = bdot(hid[0:span, :], w_ref[:, cols]).astype(BF16)
        inn[:, cols] = values
        wide = values.astype(F32)
        st_f[0, :, cols] = bdot(in_f, (bdot(tail_own, widen_f[:, cols]) * wide).astype(BF16))
        st_b[0, :, cols] = bdot(in_b, (bdot(tail_own, widen_b[:, cols]) * wide).astype(BF16))
        return carry

    lax.fori_loop(0, tiles, project_own, 0)

    out_f = maps[:, states : 2 * states]
    out_b = maps[:, 3 * states :]
    own_out[0] = out_f
    own_out[1] = out_b
    own_scale[...] = halves(jnp.exp(jnp.where(is_fwd, cum, last_own - exc)))
    score = jnp.where(
        lower,
        lax.dot_general(out_f, maps[:, :states], over, preferred_element_type=F32),
        lax.dot_general(
            out_b, maps[:, 2 * states : 3 * states], over, preferred_element_type=F32
        ),
    )
    score = jnp.where(level, 0.0, score)
    unit = jnp.where(level, 1.0, 0.0).astype(F32)
    cum_line[...] = turned(cum, unit)
    exc_line[...] = turned(exc, unit)
    step_line[...] = turned(steps, unit)
    cum_two = halves(cum)
    exc_two = halves(exc)
    skip_two = halves(
        jnp.broadcast_to(jnp.concatenate([skip_ref[...], skip_ref[...]], axis=1), (8, two))
    )
    owner = lax.rem(lax.broadcasted_iota(jnp.int32, (2 * two, 128), 0), two)

    def mix(i):
        cols = columns(i, 128)
        both = inn[:, cols]
        parts = []
        for k in (2 * i, 2 * i + 1):
            pick_f = jnp.where(owner == k, 1.0, 0.0).astype(BF16)
            pick_b = jnp.where(owner == k + heads, 1.0, 0.0).astype(BF16)
            fwd = pl.ds(k, 1)
            bwd = pl.ds(k + heads, 1)
            gap = jnp.where(
                lower,
                bdot(cum_two, pick_f) - cum_line[fwd, :],
                exc_line[bwd, :] - bdot(exc_two, pick_b),
            )
            scale = jnp.where(lower, step_line[fwd, :], step_line[bwd, :])
            parts.append(bdot((jnp.exp(gap) * (score * scale)).astype(BF16), both))
        gain = bdot(skip_two, widen_f[:, cols])[0:1, :]
        return jnp.where(left_half, parts[0], parts[1]) + gain * both.astype(F32)

    lasts = [last_own]

    def arrived(d):
        for e in range(1, nh):
            sib(jnp.int32(d), e, x_ref).wait_recv()
        maps, steps, logs = prepare(hid[d * span : (d + 1) * span, :])
        _, _, last, tail = sums(steps, logs)
        lasts.append(last)
        tails[(d - 1) * span : d * span, :] = tail
        in_turn[0, d - 1] = turn(maps[:, :states])
        in_turn[1, d - 1] = turn(maps[:, 2 * states : 3 * states])

    for d in range(1, GROUP):
        if d == GROUP - 2:
            forward(jnp.int32(GROUP - 1))
        arrived(d)

    def project(k):
        cols = columns(k, chunk)
        wide = bdot(hid[span:, :], w_ref[:, cols]).astype(BF16).astype(F32)
        for way, grow, st in ((0, widen_f, st_f), (1, widen_b, st_b)):
            scaled = (bdot(tails[...], grow[:, cols]) * wide).astype(BF16)
            for d in range(1, GROUP):
                st[d, :, cols] = bdot(in_turn[way, d - 1], scaled[(d - 1) * span : d * span])

    at = [partner(jnp.int32(d)) for d in range(GROUP)]
    none = jnp.zeros_like(last_own)

    def between(keep):
        kept = [jnp.where(keep(at[c]), lasts[c], none) for c in range(GROUP)]
        return jnp.exp(sum(kept, none))

    def always(c):
        return c >= 0

    all_f = [between(lambda c, b=b: c > b) for b in at]
    all_b = [between(lambda c, b=b: c < b) for b in at]
    mine_f = [
        jnp.where(b < place, between(lambda c, b=b: (c > b) & (c < place)), none) for b in at
    ]
    mine_b = [
        jnp.where(b > place, between(lambda c, b=b: (c < b) & (c > place)), none) for b in at
    ]
    every_f = all_f + [between(always)] + mine_f + [between(lambda c: c < place)]
    every_b = all_b + [between(always)] + mine_b + [between(lambda c: c > place)]
    pad = [none] * (16 - len(every_f))
    lines[0:16] = bdot(halves(jnp.concatenate(every_f + pad, axis=0)), widen_f[...])
    lines[16:32] = bdot(halves(jnp.concatenate(every_b + pad, axis=0)), widen_b[...])

    def f_copy(k):
        return pltpu.make_async_remote_copy(
            src_ref=snd_f.at[k], dst_ref=rcv_f.at[k], send_sem=fs_sem.at[k], recv_sem=fr_sem.at[k],
            device_id=(s + GROUP, h), device_id_type=MESH,
        )

    def b_copy(k):
        return pltpu.make_async_remote_copy(
            src_ref=snd_b.at[k], dst_ref=rcv_b.at[k], send_sem=bs_sem.at[k], recv_sem=br_sem.at[k],
            device_id=(s - GROUP, h), device_id_type=MESH,
        )

    def gathered(k, first, st, rcv):
        cols = columns(k, chunk)
        line = lines[:, cols]
        total = line[first + GROUP : first + GROUP + 1] * rcv[k].astype(F32)
        for b in range(GROUP):
            total = total + line[first + b : first + b + 1] * st[b, :, cols]
        return total.astype(BF16)

    def pass_on(k, base, st, rcv, snd, copy, got, sent):
        inside = (k >= 0) & (k < chunks)

        @pl.when(inside & got)
        def _():
            copy(k).wait_recv()

        @pl.when(inside & sent)
        def _():
            snd[k] = gathered(k, base, st, rcv)
            copy(k).start()

    lag_f = STRIDE * lap
    lag_b = STRIDE * (laps - 1 - lap)
    lag = jnp.maximum(lag_f, lag_b)

    def slot(n, carry):
        pass_on(n - lag_f, 0, st_f, rcv_f, snd_f, f_copy, lap > 0, lap < laps - 1)
        pass_on(
            n - lag_b, 16, st_b, rcv_b, snd_b, b_copy, lap < laps - 1, lap > 0
        )
        k = n - lag

        @pl.when(n < chunks - 1)
        def _():
            project(n + 1)

        @pl.when((k >= 0) & (k < chunks))
        def _():
            cols = columns(k, chunk)
            ahead = gathered(k, GROUP + 1, st_f, rcv_f)
            behind = gathered(k, 16 + GROUP + 1, st_b, rcv_b)
            scale_f = bdot(own_scale[...], widen_f[:, cols])
            scale_b = bdot(own_scale[...], widen_b[:, cols])
            pairs = chunk // 128
            local = jnp.concatenate([mix(k * pairs + i) for i in range(pairs)], axis=1)
            result = local + scale_f * bdot(own_out[0], ahead)
            result = result + scale_b * bdot(own_out[1], behind)
            out_ref[:, cols] = result.astype(out_ref.dtype)

        return carry

    project(zero)
    lax.fori_loop(0, chunks + STRIDE * (laps - 1), slot, 0)

    for d in range(1, GROUP):
        peer(jnp.int32(d)).wait_send()
    for d in range(GROUP):
        for e in range(1, nh):
            sib(jnp.int32(d), e, x_ref).wait_send()

    @pl.when(lap < laps - 1)
    def _():
        lax.fori_loop(0, chunks, lambda k, c: (f_copy(k).wait_send(), c)[1], 0)

    @pl.when(lap > 0)
    def _():
        lax.fori_loop(0, chunks, lambda k, c: (b_copy(k).wait_send(), c)[1], 0)


def shards(ns, nh, hidden_in, w_inner, w_inout, w_step, step_bias, decay_rate, skip_gain):
    rows, dim = hidden_in.shape
    width = w_inner.shape[1]
    heads = w_step.shape[2]
    states = w_inout.shape[1] // 4
    span = rows * nh
    tile = 512
    chunk = 256
    tiles, chunks = width // tile, width // chunk
    dma = pltpu.SemaphoreType.DMA
    vmem = pl.BlockSpec(memory_space=pltpu.VMEM)
    hbm = pl.BlockSpec(memory_space=pl.ANY)
    return pl.pallas_call(
        functools.partial(kernel, ns, nh, rows, dim, width, heads, states, tile, chunk),
        out_shape=jax.ShapeDtypeStruct((span, width), BF16),
        in_specs=[hbm, hbm, hbm, vmem, vmem, vmem, vmem],
        out_specs=vmem,
        scratch_shapes=[
            pltpu.VMEM((GROUP * span, dim), BF16),
            pltpu.VMEM((dim, width), BF16),
            pltpu.VMEM((dim, 4 * states), BF16),
            pltpu.VMEM((span, width), BF16),
            pltpu.VMEM((GROUP, states, width), F32),
            pltpu.VMEM((GROUP, states, width), F32),
            pltpu.VMEM((2, span, states), BF16),
            pltpu.VMEM((span, 4 * heads), BF16),
            pltpu.VMEM((4 * heads, width), BF16),
            pltpu.VMEM((4 * heads, width), BF16),
            pltpu.VMEM((32, width), F32),
            pltpu.VMEM((2 * heads, span), F32),
            pltpu.VMEM((2 * heads, span), F32),
            pltpu.VMEM((2 * heads, span), F32),
            pltpu.VMEM(((GROUP - 1) * span, 4 * heads), BF16),
            pltpu.VMEM((2, GROUP - 1, states, span), BF16),
            pltpu.VMEM((chunks, states, chunk), BF16),
            pltpu.VMEM((chunks, states, chunk), BF16),
            pltpu.VMEM((chunks, states, chunk), BF16),
            pltpu.VMEM((chunks, states, chunk), BF16),
            dma((tiles,)),
            dma,
            dma,
            dma((GROUP - 1,)),
            dma((GROUP - 1,)),
            dma((GROUP * (nh - 1),)),
            dma((GROUP * (nh - 1),)),
            dma((chunks,)),
            dma((chunks,)),
            dma((chunks,)),
            dma((chunks,)),
        ],
        compiler_params=pltpu.CompilerParams(
            collective_id=0, has_side_effects=True, vmem_limit_bytes=56 * 1024 * 1024
        ),
    )(
        hidden_in, w_inner, w_inout,
        jnp.swapaxes(w_step, 1, 2).reshape(2 * heads, dim), step_bias,
        decay_rate.reshape(1, heads), skip_gain.reshape(1, heads),
    )


def solution(mesh):
    placed = (
        P(("seq", "head"), None),
        P(None, "head"),
        P(),
        P(None, None, "head"),
        P(None, "head"),
        P("head"),
        P("head"),
    )
    return jax.shard_map(
        functools.partial(shards, mesh.shape["seq"], mesh.shape["head"]),
        mesh=mesh, in_specs=placed, out_specs=P("seq", "head"), check_vma=False,
    )
```

```python
import functools

import jax
import jax.numpy as jnp
from jax import lax
from jax.experimental import pallas as pl
from jax.experimental.pallas import tpu as pltpu
from jax.sharding import PartitionSpec as P

HEADDIM = 64
GROUP = 4
STRIDE = 2
MESH = pl.DeviceIdType.MESH
F32 = jnp.float32
BF16 = jnp.bfloat16
EXACT = lax.Precision.HIGHEST


def bdot(a, b):
    return jnp.dot(a, b, preferred_element_type=F32)


def turned(a, b):
    return lax.dot_general(
        a, b, (((0,), (0,)), ((), ())), precision=EXACT, preferred_element_type=F32
    )


def softplus(x):
    return jnp.maximum(x, 0.0) + jnp.log1p(jnp.exp(-jnp.abs(x)))


def halves(x):
    top = x.astype(BF16).astype(F32)
    return jnp.concatenate([top, x - top], axis=1).astype(BF16)


def kernel(
    ns, nh, rows, dim, width, heads, states, tile, chunk,
    x_ref, w_hbm, wio_hbm, ws_ref, bias_ref, rate_ref, skip_ref, out_ref,
    hid, w_ref, wio_ref, inn, st_f, st_b, own_out, own_scale,
    widen_f, widen_b, lines, cum_line, exc_line, step_line, tails, in_turn,
    snd_f, snd_b, rcv_f, rcv_b,
    w_sem, wio_sem, x_sem, peer_send, peer_recv, sib_send, sib_recv,
    fs_sem, fr_sem, bs_sem, br_sem, fshare_sem, bshare_sem,
):
    s = lax.axis_index("seq")
    h = lax.axis_index("head")
    span = rows * nh
    place = lax.rem(s, GROUP)
    lap = lax.div(s, GROUP)
    laps = ns // GROUP
    first_seq = s - place
    tiles = width // tile
    chunks = width // chunk

    def partner(d):
        px = lax.rem(lax.rem(place, 2) + lax.rem(d, 2), 2)
        py = lax.rem(lax.div(place, 2) + lax.div(d, 2), 2)
        return py * 2 + px

    def sibling(e):
        return lax.rem(h + e, nh)

    def piece(d, hh):
        return pl.ds(pl.multiple_of((d * nh + hh) * rows, rows), rows)

    def columns(t, size):
        return pl.ds(pl.multiple_of(t * size, size), size)

    def w_copy(t):
        return pltpu.make_async_copy(
            w_hbm.at[:, columns(t, tile)], w_ref.at[:, columns(t, tile)], w_sem.at[t]
        )

    own_copy = pltpu.make_async_copy(x_ref, hid.at[piece(0, h)], x_sem)
    own_copy.start()
    wio_copy = pltpu.make_async_copy(wio_hbm, wio_ref, wio_sem)
    wio_copy.start()
    for t in range(tiles):
        w_copy(jnp.int32(t)).start()

    barrier = pltpu.get_barrier_semaphore()
    for d in range(1, GROUP):
        to = first_seq + partner(jnp.int32(d))
        pl.semaphore_signal(barrier, 1, device_id=(to, h), device_id_type=MESH)
    for e in range(1, nh):
        pl.semaphore_signal(barrier, 1, device_id=(s, sibling(e)), device_id_type=MESH)

    @pl.when(lap > 0)
    def _():
        pl.semaphore_signal(barrier, 1, device_id=(s - GROUP, h), device_id_type=MESH)

    @pl.when(lap < laps - 1)
    def _():
        pl.semaphore_signal(barrier, 1, device_id=(s + GROUP, h), device_id_type=MESH)

    near = jnp.where(lap > 0, 1, 0) + jnp.where(lap < laps - 1, 1, 0)
    pl.semaphore_wait(barrier, GROUP - 1 + nh - 1 + near)

    def peer(d, src=x_ref, to=None):
        return pltpu.make_async_remote_copy(
            src_ref=src,
            dst_ref=hid.at[piece(d, h)],
            send_sem=peer_send.at[d - 1],
            recv_sem=peer_recv.at[d - 1],
            device_id=(first_seq + partner(d if to is None else to), h),
            device_id_type=MESH,
        )

    def relay():
        first = 1 + lax.rem(h, 2)
        peer(first).wait_recv()
        peer(jnp.int32(3), hid.at[piece(first, h)], 3 - first).start()
        second = 3 - first
        peer(second).wait_recv()
        for d in (first, second):
            for e in range(1, nh):
                sib(d, e, hid.at[piece(d, h)]).start()

    def sib(d, e, src):
        return pltpu.make_async_remote_copy(
            src_ref=src,
            dst_ref=hid.at[piece(d, h)],
            send_sem=sib_send.at[d * (nh - 1) + e - 1],
            recv_sem=sib_recv.at[d * (nh - 1) + e - 1],
            device_id=(s, sibling(e)),
            device_id_type=MESH,
        )

    zero = jnp.int32(0)
    for e in range(1, nh):
        sib(zero, e, x_ref).start()
    for d in (1, 2):
        peer(jnp.int32(d)).start()

    @pl.when(lap == 0)
    def _():
        rcv_f[...] = jnp.zeros_like(rcv_f)

    @pl.when(lap == laps - 1)
    def _():
        rcv_b[...] = jnp.zeros_like(rcv_b)

    below = lax.broadcasted_iota(jnp.int32, (span, span), 0)
    right = lax.broadcasted_iota(jnp.int32, (span, span), 1)
    left_half = lax.broadcasted_iota(jnp.int32, (1, 128), 1) < HEADDIM
    lower = below > right
    level = below == right
    tri = jnp.where(below >= right, 1.0, 0.0).astype(F32)
    over = (((1,), (1,)), ((), ()))
    rate = jnp.concatenate([rate_ref[...], rate_ref[...]], axis=1)
    bias = jnp.concatenate([bias_ref[0:1, :], bias_ref[1:2, :]], axis=1)
    two = 2 * heads
    is_fwd = lax.broadcasted_iota(jnp.int32, (span, two), 1) < heads

    part = lax.rem(lax.broadcasted_iota(jnp.int32, (2 * two, width), 0), two) * HEADDIM
    column = lax.broadcasted_iota(jnp.int32, (2 * two, width), 1)
    widen_f[...] = jnp.where((column >= part) & (column < part + HEADDIM), 1.0, 0.0).astype(BF16)
    part = part - width
    widen_b[...] = jnp.where((column >= part) & (column < part + HEADDIM), 1.0, 0.0).astype(BF16)

    def forward(d):
        peer(d).wait_recv()
        for e in range(1, nh):
            sib(d, e, hid.at[piece(d, h)]).start()

    def prepare(xb):
        maps = bdot(xb, wio_ref[...]).astype(BF16)
        steps = softplus(
            lax.dot_general(xb, ws_ref[...], over, preferred_element_type=F32) + bias
        )
        return maps, steps, -rate * steps

    def sums(steps, logs):
        cum = jnp.dot(tri, logs, precision=EXACT, preferred_element_type=F32)
        exc = cum - logs
        last = cum[span - 1 : span, :]
        tail = jnp.exp(jnp.where(is_fwd, last - cum, exc)) * steps
        return cum, exc, last, halves(tail)

    def turn(m):
        return m.astype(F32).T.astype(BF16)

    own_copy.wait()
    for e in range(1, nh):
        sib(zero, e, x_ref).wait_recv()
    wio_copy.wait()
    maps, steps, logs = prepare(hid[0:span, :])
    relay()
    cum, exc, last_own, tail_own = sums(steps, logs)
    in_f = turn(maps[:, :states])
    in_b = turn(maps[:, 2 * states : 3 * states])

    def project_own(t, carry):
        cols = columns(t, tile)
        w_copy(t).wait()
        values = bdot(hid[0:span, :], w_ref[:, cols]).astype(BF16)
        inn[:, cols] = values
        wide = values.astype(F32)
        st_f[0, :, cols] = bdot(in_f, (bdot(tail_own, widen_f[:, cols]) * wide).astype(BF16))
        st_b[0, :, cols] = bdot(in_b, (bdot(tail_own, widen_b[:, cols]) * wide).astype(BF16))
        return carry

    lax.fori_loop(0, tiles, project_own, 0)

    out_f = maps[:, states : 2 * states]
    out_b = maps[:, 3 * states :]
    own_out[0] = out_f
    own_out[1] = out_b
    own_scale[...] = halves(jnp.exp(jnp.where(is_fwd, cum, last_own - exc)))
    score = jnp.where(
        lower,
        lax.dot_general(out_f, maps[:, :states], over, preferred_element_type=F32),
        lax.dot_general(
            out_b, maps[:, 2 * states : 3 * states], over, preferred_element_type=F32
        ),
    )
    score = jnp.where(level, 0.0, score)
    unit = jnp.where(level, 1.0, 0.0).astype(F32)
    cum_line[...] = turned(cum, unit)
    exc_line[...] = turned(exc, unit)
    step_line[...] = turned(steps, unit)
    cum_two = halves(cum)
    exc_two = halves(exc)
    skip_two = halves(
        jnp.broadcast_to(jnp.concatenate([skip_ref[...], skip_ref[...]], axis=1), (8, two))
    )
    owner = lax.rem(lax.broadcasted_iota(jnp.int32, (2 * two, 128), 0), two)

    def mix(i):
        cols = columns(i, 128)
        both = inn[:, cols]
        parts = []
        for k in (2 * i, 2 * i + 1):
            pick_f = jnp.where(owner == k, 1.0, 0.0).astype(BF16)
            pick_b = jnp.where(owner == k + heads, 1.0, 0.0).astype(BF16)
            fwd = pl.ds(k, 1)
            bwd = pl.ds(k + heads, 1)
            gap = jnp.where(
                lower,
                bdot(cum_two, pick_f) - cum_line[fwd, :],
                exc_line[bwd, :] - bdot(exc_two, pick_b),
            )
            scale = jnp.where(lower, step_line[fwd, :], step_line[bwd, :])
            parts.append(bdot((jnp.exp(gap) * (score * scale)).astype(BF16), both))
        gain = bdot(skip_two, widen_f[:, cols])[0:1, :]
        return jnp.where(left_half, parts[0], parts[1]) + gain * both.astype(F32)

    lasts = [last_own]

    def arrived(d):
        for e in range(1, nh):
            sib(jnp.int32(d), e, x_ref).wait_recv()
        maps, steps, logs = prepare(hid[d * span : (d + 1) * span, :])
        _, _, last, tail = sums(steps, logs)
        lasts.append(last)
        tails[(d - 1) * span : d * span, :] = tail
        in_turn[0, d - 1] = turn(maps[:, :states])
        in_turn[1, d - 1] = turn(maps[:, 2 * states : 3 * states])

    for d in range(1, GROUP):
        if d == GROUP - 2:
            forward(jnp.int32(GROUP - 1))
        arrived(d)

    def project(k):
        cols = columns(k, chunk)
        wide = bdot(hid[span:, :], w_ref[:, cols]).astype(BF16).astype(F32)
        for way, grow, st in ((0, widen_f, st_f), (1, widen_b, st_b)):
            scaled = (bdot(tails[...], grow[:, cols]) * wide).astype(BF16)
            for d in range(1, GROUP):
                st[d, :, cols] = bdot(in_turn[way, d - 1], scaled[(d - 1) * span : d * span])

    at = [partner(jnp.int32(d)) for d in range(GROUP)]
    none = jnp.zeros_like(last_own)

    def between(keep):
        kept = [jnp.where(keep(at[c]), lasts[c], none) for c in range(GROUP)]
        return jnp.exp(sum(kept, none))

    def always(c):
        return c >= 0

    all_f = [between(lambda c, b=b: c > b) for b in at]
    all_b = [between(lambda c, b=b: c < b) for b in at]
    mine_f = [
        jnp.where(b < place, between(lambda c, b=b: (c > b) & (c < place)), none) for b in at
    ]
    mine_b = [
        jnp.where(b > place, between(lambda c, b=b: (c < b) & (c > place)), none) for b in at
    ]
    every_f = all_f + [between(always)] + mine_f + [between(lambda c: c < place)]
    every_b = all_b + [between(always)] + mine_b + [between(lambda c: c > place)]
    pad = [none] * (16 - len(every_f))
    lines[0:16] = bdot(halves(jnp.concatenate(every_f + pad, axis=0)), widen_f[...])
    lines[16:32] = bdot(halves(jnp.concatenate(every_b + pad, axis=0)), widen_b[...])

    def f_copy(k):
        return pltpu.make_async_remote_copy(
            src_ref=snd_f.at[k], dst_ref=rcv_f.at[k], send_sem=fs_sem.at[k], recv_sem=fr_sem.at[k],
            device_id=(s + GROUP, h), device_id_type=MESH,
        )

    def b_copy(k):
        return pltpu.make_async_remote_copy(
            src_ref=snd_b.at[k], dst_ref=rcv_b.at[k], send_sem=bs_sem.at[k], recv_sem=br_sem.at[k],
            device_id=(s - GROUP, h), device_id_type=MESH,
        )

    def gathered(k, first, st, rcv):
        cols = columns(k, chunk)
        line = lines[:, cols]
        total = line[first + GROUP : first + GROUP + 1] * rcv[k].astype(F32)
        for b in range(GROUP):
            total = total + line[first + b : first + b + 1] * st[b, :, cols]
        return total.astype(BF16)

    shared = GROUP if chunks >= 2 * GROUP else 0
    direct = chunks - shared
    chained = direct + (1 if shared else 0)

    def chunk_at(p):
        if not shared:
            return p
        other = lax.rem(place + jnp.maximum(p - direct, 0), GROUP)
        return jnp.where(p == 0, place, jnp.where(p <= direct, shared + p - 1, other))

    def share(rcv, sent, got, d):
        return pltpu.make_async_remote_copy(
            src_ref=rcv.at[place],
            dst_ref=rcv.at[place],
            send_sem=sent.at[d - 1],
            recv_sem=got.at[place],
            device_id=(first_seq + partner(jnp.int32(d)), h),
            device_id_type=MESH,
        )

    def pass_on(p, base, st, rcv, snd, copy, got, sent, shared_sem, arrive_sem):
        inside = (p >= 0) & (p < chained)
        k = chunk_at(p)

        @pl.when(inside & got)
        def _():
            copy(k).wait_recv()

        if shared:

            @pl.when((p == 0) & got)
            def _():
                for d in range(1, GROUP):
                    share(rcv, shared_sem, arrive_sem, d).start()

        @pl.when(inside & sent)
        def _():
            snd[k] = gathered(k, base, st, rcv)
            copy(k).start()

    lag_f = STRIDE * lap
    lag_b = STRIDE * (laps - 1 - lap)
    lag = jnp.maximum(lag_f, lag_b)
    not_first = lap > 0
    not_last = lap < laps - 1

    def slot(n, carry):
        pass_on(
            n - lag_f, 0, st_f, rcv_f, snd_f, f_copy, not_first, not_last, fshare_sem, fr_sem
        )
        pass_on(
            n - lag_b, 16, st_b, rcv_b, snd_b, b_copy, not_last, not_first, bshare_sem, br_sem
        )
        p = n - lag

        @pl.when(n < chunks - 1)
        def _():
            project(chunk_at(n + 1))

        @pl.when((p >= 0) & (p < chunks))
        def _():
            k = chunk_at(p)

            @pl.when((p >= chained) & not_first)
            def _():
                f_copy(k).wait_recv()

            @pl.when((p >= chained) & not_last)
            def _():
                b_copy(k).wait_recv()

            cols = columns(k, chunk)
            ahead = gathered(k, GROUP + 1, st_f, rcv_f)
            behind = gathered(k, 16 + GROUP + 1, st_b, rcv_b)
            scale_f = bdot(own_scale[...], widen_f[:, cols])
            scale_b = bdot(own_scale[...], widen_b[:, cols])
            pairs = chunk // 128
            local = jnp.concatenate([mix(k * pairs + i) for i in range(pairs)], axis=1)
            result = local + scale_f * bdot(own_out[0], ahead)
            result = result + scale_b * bdot(own_out[1], behind)
            out_ref[:, cols] = result.astype(out_ref.dtype)

        return carry

    project(chunk_at(zero))
    lax.fori_loop(0, chunks + STRIDE * (laps - 1), slot, 0)

    for d in range(1, GROUP):
        peer(jnp.int32(d)).wait_send()
    for d in range(GROUP):
        for e in range(1, nh):
            sib(jnp.int32(d), e, x_ref).wait_send()

    def sent_all(copy, rcv, shared_sem, arrive_sem, got, sent):
        @pl.when(sent)
        def _():
            lax.fori_loop(0, chained, lambda p, c: (copy(chunk_at(p)).wait_send(), c)[1], 0)

        if shared:

            @pl.when(got)
            def _():
                for d in range(1, GROUP):
                    share(rcv, shared_sem, arrive_sem, d).wait_send()

    sent_all(f_copy, rcv_f, fshare_sem, fr_sem, not_first, not_last)
    sent_all(b_copy, rcv_b, bshare_sem, br_sem, not_last, not_first)


def shards(ns, nh, hidden_in, w_inner, w_inout, w_step, step_bias, decay_rate, skip_gain):
    rows, dim = hidden_in.shape
    width = w_inner.shape[1]
    heads = w_step.shape[2]
    states = w_inout.shape[1] // 4
    span = rows * nh
    tile = 512
    chunk = 256
    tiles, chunks = width // tile, width // chunk
    dma = pltpu.SemaphoreType.DMA
    vmem = pl.BlockSpec(memory_space=pltpu.VMEM)
    hbm = pl.BlockSpec(memory_space=pl.ANY)
    return pl.pallas_call(
        functools.partial(kernel, ns, nh, rows, dim, width, heads, states, tile, chunk),
        out_shape=jax.ShapeDtypeStruct((span, width), BF16),
        in_specs=[hbm, hbm, hbm, vmem, vmem, vmem, vmem],
        out_specs=vmem,
        scratch_shapes=[
            pltpu.VMEM((GROUP * span, dim), BF16),
            pltpu.VMEM((dim, width), BF16),
            pltpu.VMEM((dim, 4 * states), BF16),
            pltpu.VMEM((span, width), BF16),
            pltpu.VMEM((GROUP, states, width), F32),
            pltpu.VMEM((GROUP, states, width), F32),
            pltpu.VMEM((2, span, states), BF16),
            pltpu.VMEM((span, 4 * heads), BF16),
            pltpu.VMEM((4 * heads, width), BF16),
            pltpu.VMEM((4 * heads, width), BF16),
            pltpu.VMEM((32, width), F32),
            pltpu.VMEM((2 * heads, span), F32),
            pltpu.VMEM((2 * heads, span), F32),
            pltpu.VMEM((2 * heads, span), F32),
            pltpu.VMEM(((GROUP - 1) * span, 4 * heads), BF16),
            pltpu.VMEM((2, GROUP - 1, states, span), BF16),
            pltpu.VMEM((chunks, states, chunk), BF16),
            pltpu.VMEM((chunks, states, chunk), BF16),
            pltpu.VMEM((chunks, states, chunk), BF16),
            pltpu.VMEM((chunks, states, chunk), BF16),
            dma((tiles,)),
            dma,
            dma,
            dma((GROUP - 1,)),
            dma((GROUP - 1,)),
            dma((GROUP * (nh - 1),)),
            dma((GROUP * (nh - 1),)),
            dma((chunks,)),
            dma((chunks,)),
            dma((chunks,)),
            dma((chunks,)),
            dma((GROUP - 1,)),
            dma((GROUP - 1,)),
        ],
        compiler_params=pltpu.CompilerParams(
            collective_id=0, has_side_effects=True, vmem_limit_bytes=56 * 1024 * 1024
        ),
    )(
        hidden_in, w_inner, w_inout,
        jnp.swapaxes(w_step, 1, 2).reshape(2 * heads, dim), step_bias,
        decay_rate.reshape(1, heads), skip_gain.reshape(1, heads),
    )


def solution(mesh):
    placed = (
        P(("seq", "head"), None),
        P(None, "head"),
        P(),
        P(None, None, "head"),
        P(None, "head"),
        P("head"),
        P("head"),
    )
    return jax.shard_map(
        functools.partial(shards, mesh.shape["seq"], mesh.shape["head"]),
        mesh=mesh, in_specs=placed, out_specs=P("seq", "head"), check_vma=False,
    )
```

```python
import functools

import jax
import jax.numpy as jnp
from jax import lax
from jax.experimental import pallas as pl
from jax.experimental.pallas import tpu as pltpu
from jax.sharding import PartitionSpec as P

HEADDIM = 64
GROUP = 4
STRIDE = 2
MESH = pl.DeviceIdType.MESH
F32 = jnp.float32
BF16 = jnp.bfloat16
EXACT = lax.Precision.HIGHEST


def bdot(a, b):
    return jnp.dot(a, b, preferred_element_type=F32)


def turned(a, b):
    return lax.dot_general(
        a, b, (((0,), (0,)), ((), ())), precision=EXACT, preferred_element_type=F32
    )


def softplus(x):
    return jnp.maximum(x, 0.0) + jnp.log1p(jnp.exp(-jnp.abs(x)))


def halves(x):
    top = x.astype(BF16).astype(F32)
    return jnp.concatenate([top, x - top], axis=1).astype(BF16)


def kernel(
    ns, nh, rows, dim, width, heads, states, tile, chunk,
    x_ref, w_hbm, wio_hbm, ws_ref, bias_ref, rate_ref, skip_ref, out_ref,
    hid, w_ref, wio_ref, inn, st_f, st_b, own_out, own_scale,
    widen_f, widen_b, lines, cum_line, exc_line, step_line, tails, in_turn,
    snd_f, snd_b, rcv_f, rcv_b,
    w_sem, wio_sem, x_sem, peer_send, peer_recv, sib_send, sib_recv,
    fs_sem, fr_sem, bs_sem, br_sem, fshare_sem, bshare_sem,
):
    s = lax.axis_index("seq")
    h = lax.axis_index("head")
    span = rows * nh
    place = lax.rem(s, GROUP)
    lap = lax.div(s, GROUP)
    laps = ns // GROUP
    first_seq = s - place
    tiles = width // tile
    chunks = width // chunk

    def partner(d):
        px = lax.rem(lax.rem(place, 2) + lax.rem(d, 2), 2)
        py = lax.rem(lax.div(place, 2) + lax.div(d, 2), 2)
        return py * 2 + px

    def sibling(e):
        return lax.rem(h + e, nh)

    def piece(d, hh):
        return pl.ds(pl.multiple_of((d * nh + hh) * rows, rows), rows)

    def columns(t, size):
        return pl.ds(pl.multiple_of(t * size, size), size)

    def w_copy(t):
        return pltpu.make_async_copy(
            w_hbm.at[:, columns(t, tile)], w_ref.at[:, columns(t, tile)], w_sem.at[t]
        )

    own_copy = pltpu.make_async_copy(x_ref, hid.at[piece(0, h)], x_sem)
    own_copy.start()
    wio_copy = pltpu.make_async_copy(wio_hbm, wio_ref, wio_sem)
    wio_copy.start()
    for t in range(tiles):
        w_copy(jnp.int32(t)).start()

    barrier = pltpu.get_barrier_semaphore()
    for d in range(1, GROUP):
        to = first_seq + partner(jnp.int32(d))
        pl.semaphore_signal(barrier, 1, device_id=(to, h), device_id_type=MESH)
    for e in range(1, nh):
        pl.semaphore_signal(barrier, 1, device_id=(s, sibling(e)), device_id_type=MESH)

    @pl.when(lap > 0)
    def _():
        pl.semaphore_signal(barrier, 1, device_id=(s - GROUP, h), device_id_type=MESH)

    @pl.when(lap < laps - 1)
    def _():
        pl.semaphore_signal(barrier, 1, device_id=(s + GROUP, h), device_id_type=MESH)

    near = jnp.where(lap > 0, 1, 0) + jnp.where(lap < laps - 1, 1, 0)
    pl.semaphore_wait(barrier, GROUP - 1 + nh - 1 + near)

    def peer(d, src=x_ref, to=None):
        return pltpu.make_async_remote_copy(
            src_ref=src,
            dst_ref=hid.at[piece(d, h)],
            send_sem=peer_send.at[d - 1],
            recv_sem=peer_recv.at[d - 1],
            device_id=(first_seq + partner(d if to is None else to), h),
            device_id_type=MESH,
        )

    def relay():
        first = 1 + lax.rem(h, 2)
        peer(first).wait_recv()
        peer(jnp.int32(3), hid.at[piece(first, h)], 3 - first).start()
        second = 3 - first
        peer(second).wait_recv()
        for d in (first, second):
            for e in range(1, nh):
                sib(d, e, hid.at[piece(d, h)]).start()

    def sib(d, e, src):
        return pltpu.make_async_remote_copy(
            src_ref=src,
            dst_ref=hid.at[piece(d, h)],
            send_sem=sib_send.at[d * (nh - 1) + e - 1],
            recv_sem=sib_recv.at[d * (nh - 1) + e - 1],
            device_id=(s, sibling(e)),
            device_id_type=MESH,
        )

    zero = jnp.int32(0)
    for e in range(1, nh):
        sib(zero, e, x_ref).start()
    for d in (1, 2):
        peer(jnp.int32(d)).start()

    @pl.when(lap == 0)
    def _():
        rcv_f[...] = jnp.zeros_like(rcv_f)

    @pl.when(lap == laps - 1)
    def _():
        rcv_b[...] = jnp.zeros_like(rcv_b)

    below = lax.broadcasted_iota(jnp.int32, (span, span), 0)
    right = lax.broadcasted_iota(jnp.int32, (span, span), 1)
    left_half = lax.broadcasted_iota(jnp.int32, (1, 128), 1) < HEADDIM
    lower = below > right
    level = below == right
    tri = jnp.where(below >= right, 1.0, 0.0).astype(F32)
    over = (((1,), (1,)), ((), ()))
    rate = jnp.concatenate([rate_ref[...], rate_ref[...]], axis=1)
    bias = jnp.concatenate([bias_ref[0:1, :], bias_ref[1:2, :]], axis=1)
    two = 2 * heads
    is_fwd = lax.broadcasted_iota(jnp.int32, (span, two), 1) < heads

    part = lax.rem(lax.broadcasted_iota(jnp.int32, (2 * two, width), 0), two) * HEADDIM
    column = lax.broadcasted_iota(jnp.int32, (2 * two, width), 1)
    widen_f[...] = jnp.where((column >= part) & (column < part + HEADDIM), 1.0, 0.0).astype(BF16)
    part = part - width
    widen_b[...] = jnp.where((column >= part) & (column < part + HEADDIM), 1.0, 0.0).astype(BF16)

    def forward(d):
        peer(d).wait_recv()
        for e in range(1, nh):
            sib(d, e, hid.at[piece(d, h)]).start()

    def prepare(xb):
        maps = bdot(xb, wio_ref[...]).astype(BF16)
        steps = softplus(
            lax.dot_general(xb, ws_ref[...], over, preferred_element_type=F32) + bias
        )
        return maps, steps, -rate * steps

    def sums(steps, logs):
        cum = jnp.dot(tri, logs, precision=EXACT, preferred_element_type=F32)
        exc = cum - logs
        last = cum[span - 1 : span, :]
        tail = jnp.exp(jnp.where(is_fwd, last - cum, exc)) * steps
        return cum, exc, last, halves(tail)

    def turn(m):
        return m.astype(F32).T.astype(BF16)

    own_copy.wait()
    for e in range(1, nh):
        sib(zero, e, x_ref).wait_recv()
    wio_copy.wait()
    maps, steps, logs = prepare(hid[0:span, :])
    relay()
    cum, exc, last_own, tail_own = sums(steps, logs)
    tails[0:span, :] = tail_own
    in_turn[0, 0] = turn(maps[:, :states])
    in_turn[1, 0] = turn(maps[:, 2 * states : 3 * states])

    out_f = maps[:, states : 2 * states]
    out_b = maps[:, 3 * states :]
    own_out[0] = out_f
    own_out[1] = out_b
    own_scale[...] = halves(jnp.exp(jnp.where(is_fwd, cum, last_own - exc)))
    score = jnp.where(
        lower,
        lax.dot_general(out_f, maps[:, :states], over, preferred_element_type=F32),
        lax.dot_general(
            out_b, maps[:, 2 * states : 3 * states], over, preferred_element_type=F32
        ),
    )
    score = jnp.where(level, 0.0, score)
    unit = jnp.where(level, 1.0, 0.0).astype(F32)
    cum_line[...] = turned(cum, unit)
    exc_line[...] = turned(exc, unit)
    step_line[...] = turned(steps, unit)
    cum_two = halves(cum)
    exc_two = halves(exc)
    skip_two = halves(
        jnp.broadcast_to(jnp.concatenate([skip_ref[...], skip_ref[...]], axis=1), (8, two))
    )
    owner = lax.rem(lax.broadcasted_iota(jnp.int32, (2 * two, 128), 0), two)

    def mix(i):
        cols = columns(i, 128)
        both = inn[:, cols]
        parts = []
        for k in (2 * i, 2 * i + 1):
            pick_f = jnp.where(owner == k, 1.0, 0.0).astype(BF16)
            pick_b = jnp.where(owner == k + heads, 1.0, 0.0).astype(BF16)
            fwd = pl.ds(k, 1)
            bwd = pl.ds(k + heads, 1)
            gap = jnp.where(
                lower,
                bdot(cum_two, pick_f) - cum_line[fwd, :],
                exc_line[bwd, :] - bdot(exc_two, pick_b),
            )
            scale = jnp.where(lower, step_line[fwd, :], step_line[bwd, :])
            parts.append(bdot((jnp.exp(gap) * (score * scale)).astype(BF16), both))
        gain = bdot(skip_two, widen_f[:, cols])[0:1, :]
        return jnp.where(left_half, parts[0], parts[1]) + gain * both.astype(F32)

    lasts = [last_own]

    def arrived(d):
        for e in range(1, nh):
            sib(jnp.int32(d), e, x_ref).wait_recv()
        maps, steps, logs = prepare(hid[d * span : (d + 1) * span, :])
        _, _, last, tail = sums(steps, logs)
        lasts.append(last)
        tails[d * span : (d + 1) * span, :] = tail
        in_turn[0, d] = turn(maps[:, :states])
        in_turn[1, d] = turn(maps[:, 2 * states : 3 * states])

    for d in range(1, GROUP):
        if d == GROUP - 2:
            forward(jnp.int32(GROUP - 1))
        arrived(d)

    def project(k):
        cols = columns(k, chunk)
        values = bdot(hid[...], w_ref[:, cols]).astype(BF16)
        inn[:, cols] = values[0:span]
        wide = values.astype(F32)
        for way, grow, st in ((0, widen_f, st_f), (1, widen_b, st_b)):
            scaled = (bdot(tails[...], grow[:, cols]) * wide).astype(BF16)
            for d in range(GROUP):
                st[d, :, cols] = bdot(in_turn[way, d], scaled[d * span : (d + 1) * span])

    at = [partner(jnp.int32(d)) for d in range(GROUP)]
    none = jnp.zeros_like(last_own)

    def between(keep):
        kept = [jnp.where(keep(at[c]), lasts[c], none) for c in range(GROUP)]
        return jnp.exp(sum(kept, none))

    def always(c):
        return c >= 0

    all_f = [between(lambda c, b=b: c > b) for b in at]
    all_b = [between(lambda c, b=b: c < b) for b in at]
    mine_f = [
        jnp.where(b < place, between(lambda c, b=b: (c > b) & (c < place)), none) for b in at
    ]
    mine_b = [
        jnp.where(b > place, between(lambda c, b=b: (c < b) & (c > place)), none) for b in at
    ]
    every_f = all_f + [between(always)] + mine_f + [between(lambda c: c < place)]
    every_b = all_b + [between(always)] + mine_b + [between(lambda c: c > place)]
    pad = [none] * (16 - len(every_f))
    lines[0:16] = bdot(halves(jnp.concatenate(every_f + pad, axis=0)), widen_f[...])
    lines[16:32] = bdot(halves(jnp.concatenate(every_b + pad, axis=0)), widen_b[...])

    def f_copy(k):
        return pltpu.make_async_remote_copy(
            src_ref=snd_f.at[k], dst_ref=rcv_f.at[k], send_sem=fs_sem.at[k], recv_sem=fr_sem.at[k],
            device_id=(s + GROUP, h), device_id_type=MESH,
        )

    def b_copy(k):
        return pltpu.make_async_remote_copy(
            src_ref=snd_b.at[k], dst_ref=rcv_b.at[k], send_sem=bs_sem.at[k], recv_sem=br_sem.at[k],
            device_id=(s - GROUP, h), device_id_type=MESH,
        )

    def gathered(k, first, st, rcv):
        cols = columns(k, chunk)
        line = lines[:, cols]
        total = line[first + GROUP : first + GROUP + 1] * rcv[k].astype(F32)
        for b in range(GROUP):
            total = total + line[first + b : first + b + 1] * st[b, :, cols]
        return total.astype(BF16)

    shared = GROUP if chunks >= 2 * GROUP else 0
    direct = chunks - shared
    chained = direct + (1 if shared else 0)

    def chunk_at(p):
        if not shared:
            return p
        other = lax.rem(place + jnp.maximum(p - direct, 0), GROUP)
        return jnp.where(p == 0, place, jnp.where(p <= direct, shared + p - 1, other))

    def share(rcv, sent, got, d):
        return pltpu.make_async_remote_copy(
            src_ref=rcv.at[place],
            dst_ref=rcv.at[place],
            send_sem=sent.at[d - 1],
            recv_sem=got.at[place],
            device_id=(first_seq + partner(jnp.int32(d)), h),
            device_id_type=MESH,
        )

    def pass_on(p, base, st, rcv, snd, copy, got, sent, shared_sem, arrive_sem):
        inside = (p >= 0) & (p < chained)
        k = chunk_at(p)

        @pl.when(inside & got)
        def _():
            copy(k).wait_recv()

        if shared:

            @pl.when((p == 0) & got)
            def _():
                for d in range(1, GROUP):
                    share(rcv, shared_sem, arrive_sem, d).start()

        @pl.when(inside & sent)
        def _():
            snd[k] = gathered(k, base, st, rcv)
            copy(k).start()

    lag_f = STRIDE * lap
    lag_b = STRIDE * (laps - 1 - lap)
    lag = jnp.maximum(lag_f, lag_b)
    not_first = lap > 0
    not_last = lap < laps - 1

    def slot(n, carry):
        pass_on(
            n - lag_f, 0, st_f, rcv_f, snd_f, f_copy, not_first, not_last, fshare_sem, fr_sem
        )
        pass_on(
            n - lag_b, 16, st_b, rcv_b, snd_b, b_copy, not_last, not_first, bshare_sem, br_sem
        )
        p = n - lag

        @pl.when(n < chunks - 1)
        def _():
            project(chunk_at(n + 1))

        @pl.when((p >= 0) & (p < chunks))
        def _():
            k = chunk_at(p)

            @pl.when((p >= chained) & not_first)
            def _():
                f_copy(k).wait_recv()

            @pl.when((p >= chained) & not_last)
            def _():
                b_copy(k).wait_recv()

            cols = columns(k, chunk)
            ahead = gathered(k, GROUP + 1, st_f, rcv_f)
            behind = gathered(k, 16 + GROUP + 1, st_b, rcv_b)
            scale_f = bdot(own_scale[...], widen_f[:, cols])
            scale_b = bdot(own_scale[...], widen_b[:, cols])
            pairs = chunk // 128
            local = jnp.concatenate([mix(k * pairs + i) for i in range(pairs)], axis=1)
            result = local + scale_f * bdot(own_out[0], ahead)
            result = result + scale_b * bdot(own_out[1], behind)
            out_ref[:, cols] = result.astype(out_ref.dtype)

        return carry

    for t in range(tiles):
        w_copy(jnp.int32(t)).wait()
    project(chunk_at(zero))
    lax.fori_loop(0, chunks + STRIDE * (laps - 1), slot, 0)

    for d in range(1, GROUP):
        peer(jnp.int32(d)).wait_send()
    for d in range(GROUP):
        for e in range(1, nh):
            sib(jnp.int32(d), e, x_ref).wait_send()

    def sent_all(copy, rcv, shared_sem, arrive_sem, got, sent):
        @pl.when(sent)
        def _():
            lax.fori_loop(0, chained, lambda p, c: (copy(chunk_at(p)).wait_send(), c)[1], 0)

        if shared:

            @pl.when(got)
            def _():
                for d in range(1, GROUP):
                    share(rcv, shared_sem, arrive_sem, d).wait_send()

    sent_all(f_copy, rcv_f, fshare_sem, fr_sem, not_first, not_last)
    sent_all(b_copy, rcv_b, bshare_sem, br_sem, not_last, not_first)


def shards(ns, nh, hidden_in, w_inner, w_inout, w_step, step_bias, decay_rate, skip_gain):
    rows, dim = hidden_in.shape
    width = w_inner.shape[1]
    heads = w_step.shape[2]
    states = w_inout.shape[1] // 4
    span = rows * nh
    tile = 512
    chunk = 256
    tiles, chunks = width // tile, width // chunk
    dma = pltpu.SemaphoreType.DMA
    vmem = pl.BlockSpec(memory_space=pltpu.VMEM)
    hbm = pl.BlockSpec(memory_space=pl.ANY)
    return pl.pallas_call(
        functools.partial(kernel, ns, nh, rows, dim, width, heads, states, tile, chunk),
        out_shape=jax.ShapeDtypeStruct((span, width), BF16),
        in_specs=[hbm, hbm, hbm, vmem, vmem, vmem, vmem],
        out_specs=vmem,
        scratch_shapes=[
            pltpu.VMEM((GROUP * span, dim), BF16),
            pltpu.VMEM((dim, width), BF16),
            pltpu.VMEM((dim, 4 * states), BF16),
            pltpu.VMEM((span, width), BF16),
            pltpu.VMEM((GROUP, states, width), F32),
            pltpu.VMEM((GROUP, states, width), F32),
            pltpu.VMEM((2, span, states), BF16),
            pltpu.VMEM((span, 4 * heads), BF16),
            pltpu.VMEM((4 * heads, width), BF16),
            pltpu.VMEM((4 * heads, width), BF16),
            pltpu.VMEM((32, width), F32),
            pltpu.VMEM((2 * heads, span), F32),
            pltpu.VMEM((2 * heads, span), F32),
            pltpu.VMEM((2 * heads, span), F32),
            pltpu.VMEM((GROUP * span, 4 * heads), BF16),
            pltpu.VMEM((2, GROUP, states, span), BF16),
            pltpu.VMEM((chunks, states, chunk), BF16),
            pltpu.VMEM((chunks, states, chunk), BF16),
            pltpu.VMEM((chunks, states, chunk), BF16),
            pltpu.VMEM((chunks, states, chunk), BF16),
            dma((tiles,)),
            dma,
            dma,
            dma((GROUP - 1,)),
            dma((GROUP - 1,)),
            dma((GROUP * (nh - 1),)),
            dma((GROUP * (nh - 1),)),
            dma((chunks,)),
            dma((chunks,)),
            dma((chunks,)),
            dma((chunks,)),
            dma((GROUP - 1,)),
            dma((GROUP - 1,)),
        ],
        compiler_params=pltpu.CompilerParams(
            collective_id=0, has_side_effects=True, vmem_limit_bytes=56 * 1024 * 1024
        ),
    )(
        hidden_in, w_inner, w_inout,
        jnp.swapaxes(w_step, 1, 2).reshape(2 * heads, dim), step_bias,
        decay_rate.reshape(1, heads), skip_gain.reshape(1, heads),
    )


def solution(mesh):
    placed = (
        P(("seq", "head"), None),
        P(None, "head"),
        P(),
        P(None, None, "head"),
        P(None, "head"),
        P("head"),
        P("head"),
    )
    return jax.shard_map(
        functools.partial(shards, mesh.shape["seq"], mesh.shape["head"]),
        mesh=mesh, in_specs=placed, out_specs=P("seq", "head"), check_vma=False,
    )
```

```python
import functools

import jax
import jax.numpy as jnp
from jax import lax
from jax.experimental import pallas as pl
from jax.experimental.pallas import tpu as pltpu
from jax.sharding import PartitionSpec as P

HEADDIM = 64
GROUP = 4
STRIDE = 2
LATER = 3
MESH = pl.DeviceIdType.MESH
F32 = jnp.float32
BF16 = jnp.bfloat16
EXACT = lax.Precision.HIGHEST


def bdot(a, b):
    return jnp.dot(a, b, preferred_element_type=F32)


def turned(a, b):
    return lax.dot_general(
        a, b, (((0,), (0,)), ((), ())), precision=EXACT, preferred_element_type=F32
    )


def softplus(x):
    return jnp.maximum(x, 0.0) + jnp.log1p(jnp.exp(-jnp.abs(x)))


def halves(x):
    top = x.astype(BF16).astype(F32)
    return jnp.concatenate([top, x - top], axis=1).astype(BF16)


def kernel(
    ns, nh, rows, dim, width, heads, states, tile, chunk,
    x_ref, w_hbm, wio_hbm, ws_ref, bias_ref, rate_ref, skip_ref, out_ref,
    hid, w_ref, wio_ref, inn, st_f, st_b, own_out, own_scale,
    widen_f, widen_b, lines, cum_line, exc_line, step_line, tails, in_turn,
    snd_f, snd_b, rcv_f, rcv_b,
    w_sem, wio_sem, x_sem, peer_send, peer_recv, sib_send, sib_recv,
    fs_sem, fr_sem, bs_sem, br_sem, fshare_sem, bshare_sem,
):
    s = lax.axis_index("seq")
    h = lax.axis_index("head")
    span = rows * nh
    place = lax.rem(s, GROUP)
    lap = lax.div(s, GROUP)
    laps = ns // GROUP
    first_seq = s - place
    tiles = width // tile
    chunks = width // chunk

    def partner(d):
        px = lax.rem(lax.rem(place, 2) + lax.rem(d, 2), 2)
        py = lax.rem(lax.div(place, 2) + lax.div(d, 2), 2)
        return py * 2 + px

    def sibling(e):
        return lax.rem(h + e, nh)

    def piece(d, hh):
        return pl.ds(pl.multiple_of((d * nh + hh) * rows, rows), rows)

    def columns(t, size):
        return pl.ds(pl.multiple_of(t * size, size), size)

    def w_copy(t):
        return pltpu.make_async_copy(
            w_hbm.at[:, columns(t, tile)], w_ref.at[:, columns(t, tile)], w_sem.at[t]
        )

    own_copy = pltpu.make_async_copy(x_ref, hid.at[piece(0, h)], x_sem)
    own_copy.start()
    wio_copy = pltpu.make_async_copy(wio_hbm, wio_ref, wio_sem)
    wio_copy.start()
    for t in range(tiles):
        w_copy(jnp.int32(t)).start()

    barrier = pltpu.get_barrier_semaphore()
    for d in range(1, GROUP):
        to = first_seq + partner(jnp.int32(d))
        pl.semaphore_signal(barrier, 1, device_id=(to, h), device_id_type=MESH)
    for e in range(1, nh):
        pl.semaphore_signal(barrier, 1, device_id=(s, sibling(e)), device_id_type=MESH)

    @pl.when(lap > 0)
    def _():
        pl.semaphore_signal(barrier, 1, device_id=(s - GROUP, h), device_id_type=MESH)

    @pl.when(lap < laps - 1)
    def _():
        pl.semaphore_signal(barrier, 1, device_id=(s + GROUP, h), device_id_type=MESH)

    near = jnp.where(lap > 0, 1, 0) + jnp.where(lap < laps - 1, 1, 0)
    pl.semaphore_wait(barrier, GROUP - 1 + nh - 1 + near)

    def peer(d, src=x_ref, to=None):
        return pltpu.make_async_remote_copy(
            src_ref=src,
            dst_ref=hid.at[piece(d, h)],
            send_sem=peer_send.at[d - 1],
            recv_sem=peer_recv.at[d - 1],
            device_id=(first_seq + partner(d if to is None else to), h),
            device_id_type=MESH,
        )

    def relay():
        first = 1 + lax.rem(h, 2)
        peer(first).wait_recv()
        peer(jnp.int32(3), hid.at[piece(first, h)], 3 - first).start()
        second = 3 - first
        peer(second).wait_recv()
        for d in (first, second):
            for e in range(1, nh):
                sib(d, e, hid.at[piece(d, h)]).start()

    def sib(d, e, src):
        return pltpu.make_async_remote_copy(
            src_ref=src,
            dst_ref=hid.at[piece(d, h)],
            send_sem=sib_send.at[d * (nh - 1) + e - 1],
            recv_sem=sib_recv.at[d * (nh - 1) + e - 1],
            device_id=(s, sibling(e)),
            device_id_type=MESH,
        )

    zero = jnp.int32(0)
    for e in range(1, nh):
        sib(zero, e, x_ref).start()
    for d in (1, 2):
        peer(jnp.int32(d)).start()

    @pl.when(lap == 0)
    def _():
        rcv_f[...] = jnp.zeros_like(rcv_f)

    @pl.when(lap == laps - 1)
    def _():
        rcv_b[...] = jnp.zeros_like(rcv_b)

    below = lax.broadcasted_iota(jnp.int32, (span, span), 0)
    right = lax.broadcasted_iota(jnp.int32, (span, span), 1)
    left_half = lax.broadcasted_iota(jnp.int32, (1, 128), 1) < HEADDIM
    lower = below > right
    level = below == right
    tri = jnp.where(below >= right, 1.0, 0.0).astype(F32)
    over = (((1,), (1,)), ((), ()))
    rate = jnp.concatenate([rate_ref[...], rate_ref[...]], axis=1)
    bias = jnp.concatenate([bias_ref[0:1, :], bias_ref[1:2, :]], axis=1)
    two = 2 * heads
    is_fwd = lax.broadcasted_iota(jnp.int32, (span, two), 1) < heads

    part = lax.rem(lax.broadcasted_iota(jnp.int32, (2 * two, width), 0), two) * HEADDIM
    column = lax.broadcasted_iota(jnp.int32, (2 * two, width), 1)
    widen_f[...] = jnp.where((column >= part) & (column < part + HEADDIM), 1.0, 0.0).astype(BF16)
    part = part - width
    widen_b[...] = jnp.where((column >= part) & (column < part + HEADDIM), 1.0, 0.0).astype(BF16)

    def forward(d):
        peer(d).wait_recv()
        for e in range(1, nh):
            sib(d, e, hid.at[piece(d, h)]).start()

    def prepare(xb):
        maps = bdot(xb, wio_ref[...]).astype(BF16)
        steps = softplus(
            lax.dot_general(xb, ws_ref[...], over, preferred_element_type=F32) + bias
        )
        return maps, steps, -rate * steps

    def sums(steps, logs):
        cum = jnp.dot(tri, logs, precision=EXACT, preferred_element_type=F32)
        exc = cum - logs
        last = cum[span - 1 : span, :]
        tail = jnp.exp(jnp.where(is_fwd, last - cum, exc)) * steps
        return cum, exc, last, halves(tail)

    def turn(m):
        return m.astype(F32).T.astype(BF16)

    own_copy.wait()
    for e in range(1, nh):
        sib(zero, e, x_ref).wait_recv()
    wio_copy.wait()
    maps, steps, logs = prepare(hid[0:span, :])
    relay()
    cum, exc, last_own, tail_own = sums(steps, logs)
    in_f = turn(maps[:, :states])
    in_b = turn(maps[:, 2 * states : 3 * states])

    def project_own(t, carry):
        cols = columns(t, tile)
        w_copy(t).wait()
        values = bdot(hid[0:span, :], w_ref[:, cols]).astype(BF16)
        inn[:, cols] = values
        wide = values.astype(F32)
        st_f[0, :, cols] = bdot(in_f, (bdot(tail_own, widen_f[:, cols]) * wide).astype(BF16))
        st_b[0, :, cols] = bdot(in_b, (bdot(tail_own, widen_b[:, cols]) * wide).astype(BF16))
        return carry

    lax.fori_loop(0, tiles, project_own, 0)

    out_f = maps[:, states : 2 * states]
    out_b = maps[:, 3 * states :]
    own_out[0] = out_f
    own_out[1] = out_b
    own_scale[...] = halves(jnp.exp(jnp.where(is_fwd, cum, last_own - exc)))
    score = jnp.where(
        lower,
        lax.dot_general(out_f, maps[:, :states], over, preferred_element_type=F32),
        lax.dot_general(
            out_b, maps[:, 2 * states : 3 * states], over, preferred_element_type=F32
        ),
    )
    score = jnp.where(level, 0.0, score)
    unit = jnp.where(level, 1.0, 0.0).astype(F32)
    cum_line[...] = turned(cum, unit)
    exc_line[...] = turned(exc, unit)
    step_line[...] = turned(steps, unit)
    cum_two = halves(cum)
    exc_two = halves(exc)
    skip_two = halves(
        jnp.broadcast_to(jnp.concatenate([skip_ref[...], skip_ref[...]], axis=1), (8, two))
    )
    owner = lax.rem(lax.broadcasted_iota(jnp.int32, (2 * two, 128), 0), two)

    def mix(i):
        cols = columns(i, 128)
        both = inn[:, cols]
        parts = []
        for k in (2 * i, 2 * i + 1):
            pick_f = jnp.where(owner == k, 1.0, 0.0).astype(BF16)
            pick_b = jnp.where(owner == k + heads, 1.0, 0.0).astype(BF16)
            fwd = pl.ds(k, 1)
            bwd = pl.ds(k + heads, 1)
            gap = jnp.where(
                lower,
                bdot(cum_two, pick_f) - cum_line[fwd, :],
                exc_line[bwd, :] - bdot(exc_two, pick_b),
            )
            scale = jnp.where(lower, step_line[fwd, :], step_line[bwd, :])
            parts.append(bdot((jnp.exp(gap) * (score * scale)).astype(BF16), both))
        gain = bdot(skip_two, widen_f[:, cols])[0:1, :]
        return jnp.where(left_half, parts[0], parts[1]) + gain * both.astype(F32)

    lasts = [last_own]

    def arrived(d):
        for e in range(1, nh):
            sib(jnp.int32(d), e, x_ref).wait_recv()
        maps, steps, logs = prepare(hid[d * span : (d + 1) * span, :])
        _, _, last, tail = sums(steps, logs)
        lasts.append(last)
        tails[(d - 1) * span : d * span, :] = tail
        in_turn[0, d - 1] = turn(maps[:, :states])
        in_turn[1, d - 1] = turn(maps[:, 2 * states : 3 * states])

    for d in range(1, GROUP):
        if d == GROUP - 2:
            forward(jnp.int32(GROUP - 1))
        arrived(d)

    def project(k):
        cols = columns(k, chunk)
        wide = bdot(hid[span:, :], w_ref[:, cols]).astype(BF16).astype(F32)
        for way, grow, st in ((0, widen_f, st_f), (1, widen_b, st_b)):
            scaled = (bdot(tails[...], grow[:, cols]) * wide).astype(BF16)
            for d in range(1, GROUP):
                st[d, :, cols] = bdot(in_turn[way, d - 1], scaled[(d - 1) * span : d * span])

    at = [partner(jnp.int32(d)) for d in range(GROUP)]
    none = jnp.zeros_like(last_own)

    def between(keep):
        kept = [jnp.where(keep(at[c]), lasts[c], none) for c in range(GROUP)]
        return jnp.exp(sum(kept, none))

    def always(c):
        return c >= 0

    all_f = [between(lambda c, b=b: c > b) for b in at]
    all_b = [between(lambda c, b=b: c < b) for b in at]
    mine_f = [
        jnp.where(b < place, between(lambda c, b=b: (c > b) & (c < place)), none) for b in at
    ]
    mine_b = [
        jnp.where(b > place, between(lambda c, b=b: (c < b) & (c > place)), none) for b in at
    ]
    every_f = all_f + [between(always)] + mine_f + [between(lambda c: c < place)]
    every_b = all_b + [between(always)] + mine_b + [between(lambda c: c > place)]
    pad = [none] * (16 - len(every_f))
    lines[0:16] = bdot(halves(jnp.concatenate(every_f + pad, axis=0)), widen_f[...])
    lines[16:32] = bdot(halves(jnp.concatenate(every_b + pad, axis=0)), widen_b[...])

    def f_copy(k):
        return pltpu.make_async_remote_copy(
            src_ref=snd_f.at[k], dst_ref=rcv_f.at[k], send_sem=fs_sem.at[k], recv_sem=fr_sem.at[k],
            device_id=(s + GROUP, h), device_id_type=MESH,
        )

    def b_copy(k):
        return pltpu.make_async_remote_copy(
            src_ref=snd_b.at[k], dst_ref=rcv_b.at[k], send_sem=bs_sem.at[k], recv_sem=br_sem.at[k],
            device_id=(s - GROUP, h), device_id_type=MESH,
        )

    def gathered(k, first, st, rcv):
        cols = columns(k, chunk)
        line = lines[:, cols]
        total = line[first + GROUP : first + GROUP + 1] * rcv[k].astype(F32)
        for b in range(GROUP):
            total = total + line[first + b : first + b + 1] * st[b, :, cols]
        return total.astype(BF16)

    shared = GROUP if chunks >= 2 * GROUP else 0
    direct = chunks - shared
    chained = direct + (1 if shared else 0)

    def chunk_at(p):
        if not shared:
            return p
        other = lax.rem(place + jnp.maximum(p - direct, 0), GROUP)
        return jnp.where(p == 0, place, jnp.where(p <= direct, shared + p - 1, other))

    def share(rcv, sent, got, d):
        return pltpu.make_async_remote_copy(
            src_ref=rcv.at[place],
            dst_ref=rcv.at[place],
            send_sem=sent.at[d - 1],
            recv_sem=got.at[place],
            device_id=(first_seq + partner(jnp.int32(d)), h),
            device_id_type=MESH,
        )

    def pass_on(p, base, st, rcv, snd, copy, got, sent, shared_sem, arrive_sem):
        inside = (p >= 0) & (p < chained)
        k = chunk_at(p)

        @pl.when(inside & got)
        def _():
            copy(k).wait_recv()

        if shared:

            @pl.when((p == 0) & got)
            def _():
                for d in range(1, GROUP):
                    share(rcv, shared_sem, arrive_sem, d).start()

        @pl.when(inside & sent)
        def _():
            snd[k] = gathered(k, base, st, rcv)
            copy(k).start()

    lag_f = STRIDE * lap
    lag_b = STRIDE * (laps - 1 - lap)
    not_first = lap > 0
    not_last = lap < laps - 1
    later = jnp.where(not_first & not_last, LATER, 0)
    lag = jnp.maximum(lag_f, lag_b) + later

    def slot(n, carry):
        pass_on(
            n - lag_f, 0, st_f, rcv_f, snd_f, f_copy, not_first, not_last, fshare_sem, fr_sem
        )
        pass_on(
            n - lag_b, 16, st_b, rcv_b, snd_b, b_copy, not_last, not_first, bshare_sem, br_sem
        )
        p = n - lag

        @pl.when(n < chunks - 1)
        def _():
            project(chunk_at(n + 1))

        @pl.when((p >= 0) & (p < chunks))
        def _():
            k = chunk_at(p)

            @pl.when((p >= chained) & not_first)
            def _():
                f_copy(k).wait_recv()

            @pl.when((p >= chained) & not_last)
            def _():
                b_copy(k).wait_recv()

            cols = columns(k, chunk)
            ahead = gathered(k, GROUP + 1, st_f, rcv_f)
            behind = gathered(k, 16 + GROUP + 1, st_b, rcv_b)
            scale_f = bdot(own_scale[...], widen_f[:, cols])
            scale_b = bdot(own_scale[...], widen_b[:, cols])
            pairs = chunk // 128
            local = jnp.concatenate([mix(k * pairs + i) for i in range(pairs)], axis=1)
            result = local + scale_f * bdot(own_out[0], ahead)
            result = result + scale_b * bdot(own_out[1], behind)
            out_ref[:, cols] = result.astype(out_ref.dtype)

        return carry

    project(chunk_at(zero))
    lax.fori_loop(0, chunks + STRIDE * (laps - 1) + LATER, slot, 0)

    for d in range(1, GROUP):
        peer(jnp.int32(d)).wait_send()
    for d in range(GROUP):
        for e in range(1, nh):
            sib(jnp.int32(d), e, x_ref).wait_send()

    def sent_all(copy, rcv, shared_sem, arrive_sem, got, sent):
        @pl.when(sent)
        def _():
            lax.fori_loop(0, chained, lambda p, c: (copy(chunk_at(p)).wait_send(), c)[1], 0)

        if shared:

            @pl.when(got)
            def _():
                for d in range(1, GROUP):
                    share(rcv, shared_sem, arrive_sem, d).wait_send()

    sent_all(f_copy, rcv_f, fshare_sem, fr_sem, not_first, not_last)
    sent_all(b_copy, rcv_b, bshare_sem, br_sem, not_last, not_first)


def shards(ns, nh, hidden_in, w_inner, w_inout, w_step, step_bias, decay_rate, skip_gain):
    rows, dim = hidden_in.shape
    width = w_inner.shape[1]
    heads = w_step.shape[2]
    states = w_inout.shape[1] // 4
    span = rows * nh
    tile = 512
    chunk = 256
    tiles, chunks = width // tile, width // chunk
    dma = pltpu.SemaphoreType.DMA
    vmem = pl.BlockSpec(memory_space=pltpu.VMEM)
    hbm = pl.BlockSpec(memory_space=pl.ANY)
    return pl.pallas_call(
        functools.partial(kernel, ns, nh, rows, dim, width, heads, states, tile, chunk),
        out_shape=jax.ShapeDtypeStruct((span, width), BF16),
        in_specs=[hbm, hbm, hbm, vmem, vmem, vmem, vmem],
        out_specs=vmem,
        scratch_shapes=[
            pltpu.VMEM((GROUP * span, dim), BF16),
            pltpu.VMEM((dim, width), BF16),
            pltpu.VMEM((dim, 4 * states), BF16),
            pltpu.VMEM((span, width), BF16),
            pltpu.VMEM((GROUP, states, width), F32),
            pltpu.VMEM((GROUP, states, width), F32),
            pltpu.VMEM((2, span, states), BF16),
            pltpu.VMEM((span, 4 * heads), BF16),
            pltpu.VMEM((4 * heads, width), BF16),
            pltpu.VMEM((4 * heads, width), BF16),
            pltpu.VMEM((32, width), F32),
            pltpu.VMEM((2 * heads, span), F32),
            pltpu.VMEM((2 * heads, span), F32),
            pltpu.VMEM((2 * heads, span), F32),
            pltpu.VMEM(((GROUP - 1) * span, 4 * heads), BF16),
            pltpu.VMEM((2, GROUP - 1, states, span), BF16),
            pltpu.VMEM((chunks, states, chunk), BF16),
            pltpu.VMEM((chunks, states, chunk), BF16),
            pltpu.VMEM((chunks, states, chunk), BF16),
            pltpu.VMEM((chunks, states, chunk), BF16),
            dma((tiles,)),
            dma,
            dma,
            dma((GROUP - 1,)),
            dma((GROUP - 1,)),
            dma((GROUP * (nh - 1),)),
            dma((GROUP * (nh - 1),)),
            dma((chunks,)),
            dma((chunks,)),
            dma((chunks,)),
            dma((chunks,)),
            dma((GROUP - 1,)),
            dma((GROUP - 1,)),
        ],
        compiler_params=pltpu.CompilerParams(
            collective_id=0, has_side_effects=True, vmem_limit_bytes=56 * 1024 * 1024
        ),
    )(
        hidden_in, w_inner, w_inout,
        jnp.swapaxes(w_step, 1, 2).reshape(2 * heads, dim), step_bias,
        decay_rate.reshape(1, heads), skip_gain.reshape(1, heads),
    )


def solution(mesh):
    placed = (
        P(("seq", "head"), None),
        P(None, "head"),
        P(),
        P(None, None, "head"),
        P(None, "head"),
        P("head"),
        P("head"),
    )
    return jax.shard_map(
        functools.partial(shards, mesh.shape["seq"], mesh.shape["head"]),
        mesh=mesh, in_specs=placed, out_specs=P("seq", "head"), check_vma=False,
    )
```
